512 devices in a mesh: lat: 128 (over y, z, core), lon: 4 (over x).
Axes of the slice: x: 4, y: 8, z: 8, core: 2. Of those that a mesh axis runs over, the one named last changes fastest.
Arguments:
- fields: bfloat16 [1, 512, 64, 1440], P(None, 'lat', None, 'lon'), may hold values from -6 to 6
- filter_weights: bfloat16 [49, 64, 8], replicated, may hold values from -2 to 2
- filter_values: float32 [512, 49], P('lat'), may hold values from 0.03 to 0.3
- row_offsets: int32 [512, 49], P('lat'), may hold values from -3 to 3
- col_offsets: int32 [512, 49], P('lat'), may hold values from -16 to 16, as said below
- support_sizes: int32 [512], P('lat'), may hold values from 16 to 49, as said below
Outputs:
- spectrum: float32 [1, 64, 2, 256, 256], P(None, 'lon', None, 'lat')
The draws below stay inside these ranges and needn't reach their ends.
Inputs may be any that keep to these rules, and one draw needn't show every extreme that they name: `col_offsets`: column offsets of the support lie within -16 to 16. `support_sizes`: the two latitudes nearest each pole have all 49 support cells live.
All inputs are finite; a program needn't handle non-finite values.
Results may differ from the reference program's by a relative error of at most 0.0044.
Values may be sent and summed in bfloat16 or wider, within the bound.
A program may use at most 64 MiB of HBM per device.

```python
import math
import jax
import jax.numpy as jnp
from jax import lax

CHANNELS = 64
GROUP = 8
SUPPORT = 49
LAT_REACH = 3
LON_REACH = 16
NLON = 1440
DEG = 256
BATCH = 1
NLAT = 512


def polar_distance():
    index_rows = jnp.arange(NLAT, dtype=jnp.int32)
    return (jnp.minimum(index_rows, NLAT - 1 - index_rows), index_rows)


def draw_row_offsets(key, part):
    distance, index_rows = polar_distance()
    drawn = jax.random.randint(key, (NLAT, SUPPORT), -LAT_REACH, LAT_REACH + 1, dtype=jnp.int32)
    first_col = jnp.where(index_rows % 2 == 0, LAT_REACH, -LAT_REACH).astype(jnp.int32)
    return jnp.concatenate([first_col[:, None], drawn[:, 1:]], axis=1)


def draw_col_offsets(key, part):
    distance, index_rows = polar_distance()
    reach_rows = jnp.maximum(LAT_REACH, LON_REACH - distance).astype(jnp.int32)
    raw_values = jax.random.randint(key, (NLAT, SUPPORT), 0, 65536, dtype=jnp.int32)
    drawn = raw_values % (2 * reach_rows[:, None] + 1) - reach_rows[:, None]
    first_col = jnp.where(index_rows % 2 == 0, reach_rows, -reach_rows).astype(jnp.int32)
    return jnp.concatenate([first_col[:, None], drawn[:, 1:]], axis=1)


def draw_support_sizes(key, part):
    distance, index_rows = polar_distance()
    drawn = jax.random.randint(key, (NLAT,), SUPPORT // 3, SUPPORT + 1, dtype=jnp.int32)
    return jnp.where(distance < 2, SUPPORT, drawn).astype(jnp.int32)


def level_of(own_key, extent, shards, smallest, top_value):
    factor_of = 1.0
    for position, shards_of in shards:
        draws = jax.random.uniform(jax.random.fold_in(jax.random.fold_in(own_key, 6), position), (shards_of,), jnp.float32, smallest / len(shards), top_value / len(shards))
        factor_of = factor_of * jnp.repeat(jnp.exp(draws), extent[position] // shards_of).reshape((-1,) + (1,) * (len(extent) - 1 - position))
    return factor_of


def noise(stream_key, shape, spread, reach, split=(), kind=jnp.bfloat16):
    values = jax.random.normal(stream_key, shape, jnp.float32) * spread
    if len(split) > 0:
        values = level_of(stream_key, shape, split, -0.22, 0.18) * values
    return jnp.clip(values, min=-reach, max=reach).astype(kind)


def setup_inputs(seed: int = 0) -> dict:
    key_list = jax.random.split(jax.random.key(seed), 7)
    fields = noise(key_list[0], (BATCH, NLAT, CHANNELS, NLON), 1.0, 6.0, ((1, 128), (3, 4)))
    filter_weights = noise(key_list[1], (SUPPORT, CHANNELS, GROUP), GROUP ** -0.5, 2.0)
    filter_values = jnp.clip(jnp.exp(math.log(0.3) - 2.3025852 * jax.random.uniform(key_list[2], (NLAT, SUPPORT), jnp.float32) ** level_of(key_list[2], (NLAT, SUPPORT), ((0, 128),), -0.2, 0.2)), 0.03, 0.3)
    row_offsets = draw_row_offsets(jax.random.fold_in(key_list[6], 71), 0)
    col_offsets = draw_col_offsets(jax.random.fold_in(key_list[6], 71), 0)
    support_sizes = draw_support_sizes(jax.random.fold_in(key_list[6], 71), 0)
    return dict(fields=fields, filter_weights=filter_weights, filter_values=filter_values, row_offsets=row_offsets, col_offsets=col_offsets, support_sizes=support_sizes)


def recurrence(degree_now, orders):
    degree_square = degree_now * degree_now
    order_square = orders * orders
    active = degree_now > orders
    denominator = jnp.where(active, degree_square - order_square, 1.0)
    first_factor = jnp.sqrt((4.0 * degree_square - 1.0) / denominator)
    below = (degree_now - 1.0) * (degree_now - 1.0) - order_square
    second_factor = jnp.sqrt(jnp.maximum((2.0 * degree_now + 1.0) * below, 0.0) / (jnp.maximum(2.0 * degree_now - 3.0, 1.0) * denominator))
    return (first_factor, second_factor, active)

def legendre_start(degree_count, lat_count):
    orders = jnp.arange(degree_count, dtype=jnp.float32)
    factors = jnp.arange(1, degree_count, dtype=jnp.float32)
    log_steps = jnp.log((2.0 * factors - 1.0) / (2.0 * factors))
    log_product = jnp.concatenate([jnp.zeros((1,), jnp.float32), jnp.cumsum(log_steps)])
    colatitude = math.pi * (jnp.arange(lat_count, dtype=jnp.float32) + 0.5) / lat_count
    log_sine = jnp.log(jnp.sin(colatitude))
    log_diagonal = 0.5 * (jnp.log((2.0 * orders + 1.0) / (4.0 * math.pi)) + log_product)
    diagonal_start = jnp.exp(log_diagonal[None, :] + orders[None, :] * log_sine[:, None])
    return (colatitude, diagonal_start)

def legendre_table(lat_count, degree_count):
    colatitude, diagonal_start = legendre_start(degree_count, lat_count)
    cosine = jnp.cos(colatitude)[:, None]
    order_ints = jnp.arange(degree_count, dtype=jnp.int32)[None, :]
    orders = order_ints.astype(jnp.float32)

    def advance(state_pair, degree_int):
        previous, before_previous = state_pair
        first_factor, second_factor, active = recurrence(degree_int.astype(jnp.float32), orders)
        fresh = jnp.where(active, first_factor * cosine * previous - second_factor * before_previous, jnp.where(degree_int == order_ints, diagonal_start, 0.0))
        return ((fresh, previous), fresh)
    zeros_start = jnp.zeros((lat_count, degree_count), jnp.float32)
    _, table = lax.scan(advance, (zeros_start, zeros_start), jnp.arange(degree_count, dtype=jnp.int32))
    return (colatitude, table)

def fourier_table(lon_count, degree_count):
    columns = jnp.arange(lon_count, dtype=jnp.int32)[:, None]
    orders = jnp.arange(degree_count, dtype=jnp.int32)[None, :]
    phase = 2.0 * math.pi / lon_count * (columns * orders % lon_count).astype(jnp.float32)
    return jnp.concatenate([jnp.cos(phase), -jnp.sin(phase)], axis=1).astype(jnp.bfloat16)

def reference(fields, filter_weights, filter_values, row_offsets, col_offsets, support_sizes):
    samples = fields.shape[0]
    groups = CHANNELS // GROUP
    live = (jnp.arange(SUPPORT, dtype=jnp.int32)[None, :] < support_sizes[:, None]).astype(jnp.float32)
    scaled = filter_values * live
    effective = (scaled[:, :, None, None] * filter_weights.astype(jnp.float32)[None]).astype(jnp.bfloat16)
    padded = jnp.pad(fields, ((0, 0), (LAT_REACH, LAT_REACH), (0, 0), (0, 0)))
    lat_index = jnp.arange(NLAT, dtype=jnp.int32)
    lon_index = jnp.arange(NLON, dtype=jnp.int32)

    def one_cell(cell, summed):
        row_pick = lat_index + LAT_REACH + lax.dynamic_index_in_dim(row_offsets, cell, 1, keepdims=False)
        picked = jnp.take(padded, row_pick, axis=1)
        shift = (lon_index[None, :] + lax.dynamic_index_in_dim(col_offsets, cell, 1, keepdims=False)[:, None]) % NLON
        picked = jnp.take_along_axis(picked, jnp.broadcast_to(shift[None, :, None, :], picked.shape), axis=3)
        grouped = picked.reshape(samples, NLAT, groups, GROUP, NLON).astype(jnp.float32)
        cell_weight = lax.dynamic_index_in_dim(effective, cell, 1, keepdims=False)
        cell_weight = cell_weight.reshape(NLAT, groups, GROUP, GROUP).astype(jnp.float32)
        return summed + jnp.einsum('igoa,bigaj->bigoj', cell_weight, grouped)
    summed = lax.fori_loop(0, SUPPORT, one_cell, jnp.zeros((samples, NLAT, groups, GROUP, NLON), jnp.float32))
    convolved = summed.reshape(samples, NLAT, CHANNELS, NLON).astype(jnp.bfloat16)
    fourier = fourier_table(NLON, DEG)
    zonal = jnp.dot(convolved.reshape(-1, NLON), fourier, preferred_element_type=jnp.float32)
    zonal = zonal.reshape(samples, NLAT, CHANNELS, 2, DEG)
    colatitude, table = legendre_table(NLAT, DEG)
    weighted = table * (math.pi / NLAT * jnp.sin(colatitude))[None, :, None]
    return jnp.einsum('lim,bicpm->bcpml', weighted, zonal, precision=lax.Precision.HIGHEST)
```

```python
import functools
import math

import jax
import jax.numpy as jnp
import ml_dtypes
import numpy as np
from jax import lax
from jax.experimental import pallas as pl
from jax.experimental.pallas import tpu as pltpu
from jax.sharding import PartitionSpec as P

GROUP = 8
SUPPORT = 49
LAT_REACH = 3
LON_REACH = 16
ROWS = 2 * LAT_REACH + 1
HALF = 64
ZC = 16
MESH = pl.DeviceIdType.MESH
NT = (((1,), (1,)), ((), ()))


def split(x):
    high = x.astype(ml_dtypes.bfloat16)
    low = (x - high.astype(np.float64)).astype(ml_dtypes.bfloat16)
    return high, low


def tables(lat_parts, lon_parts, lon_dev, lat_dev):
    nlon, nlat, deg = lon_parts * lon_dev, lat_parts * lat_dev, 2 * lat_parts
    orders = np.arange(deg)
    phase = 2.0 * math.pi / nlon * ((np.arange(nlon)[:, None] * orders[None, :]) % nlon)
    fourier = np.concatenate([np.cos(phase), -np.sin(phase)], 1).astype(ml_dtypes.bfloat16)
    fourier = fourier.reshape(lon_parts, lon_dev, 2 * deg)
    shifts = np.arange(-LON_REACH, LON_REACH + 1)
    turn = 2.0 * math.pi / nlon * ((orders[:, None] * shifts[None, :]) % nlon)
    turn = np.concatenate([np.cos(turn), np.sin(turn)], 0)
    shift_table = np.zeros((2 * deg, 2 * HALF), ml_dtypes.bfloat16)
    shift_table[:, : shifts.size], shift_table[:, HALF : HALF + shifts.size] = split(turn)
    y_count = lat_parts // ZC
    lane = np.arange(lat_parts)
    band = (lane % y_count) * ZC + lane // y_count
    lats = lat_dev * band[None, :] + (np.arange(8) % lat_dev)[:, None]
    colat = math.pi * (lats + 0.5) / nlat
    per_lat = np.stack([np.cos(colat), np.log(np.sin(colat)), math.pi / nlat * np.sin(colat)])
    factors = np.arange(1, deg)
    log_product = np.concatenate([[0.0], np.cumsum(np.log((2.0 * factors - 1) / (2.0 * factors)))])
    log_norm = 0.5 * (np.log((2.0 * orders + 1) / (4 * math.pi)) + log_product)
    grow = np.sqrt(np.maximum(4.0 * orders * orders - 1, 1.0))
    scalars = np.concatenate([grow, 1.0 / grow, log_norm])
    return fourier, shift_table, per_lat.astype(np.float32), scalars.astype(np.float32)


def kernel(
    fields, weights, values, row_off, col_off, sizes, fourier, shift_table, per_lat, scalars,
    out,
    blocks, four, shift, xs, meta_v, meta_r, meta_c, left, w, acc, z, send_a, recv_a, wide_a, send_b, recv_b,
    table, tcat,
    sem_in, sem_lon_s, sem_lon_r, sem_halo_s, sem_halo_r, sem_a_s, sem_a_r, sem_b_s, sem_b_r,
):
    lat, lon = lax.axis_index("lat"), lax.axis_index("lon")
    lat_parts, lon_parts = lax.axis_size("lat"), lax.axis_size("lon")
    y_count = lat_parts // ZC
    y, zc = lat // ZC, lat % ZC
    lat_dev, chans = blocks.shape[1], blocks.shape[2]
    deg = 2 * lat_parts
    f32, bf16 = jnp.float32, jnp.bfloat16

    barrier = pltpu.get_barrier_semaphore()
    for d in range(1, lon_parts):
        pl.semaphore_signal(barrier, 1, device_id=(lat, (lon + d) % lon_parts), device_id_type=MESH)
    for d in range(1, y_count):
        pl.semaphore_signal(
            barrier, 1, device_id=((y + d) % y_count * ZC + zc, lon), device_id_type=MESH
        )
    for d in range(1, ZC):
        pl.semaphore_signal(barrier, 1, device_id=(y * ZC + (zc + d) % ZC, lon), device_id_type=MESH)
    has_low, has_high = lat > 0, lat < lat_parts - 1

    @pl.when(has_low)
    def _():
        pl.semaphore_signal(barrier, 1, device_id=(lat - 1, lon), device_id_type=MESH)

    @pl.when(has_high)
    def _():
        pl.semaphore_signal(barrier, 1, device_id=(lat + 1, lon), device_id_type=MESH)

    get_four = pltpu.make_async_copy(fourier, four, sem_in.at[0])
    get_shift = pltpu.make_async_copy(shift_table, shift, sem_in.at[1])
    get_own = pltpu.make_async_copy(
        fields.at[:, pl.ds(lon * chans, chans), :], blocks.at[lon], sem_in.at[2]
    )
    get_own.start()
    get_shift.start()
    get_four.start()

    common = (lon_parts - 1) + (y_count - 1) + (ZC - 1)

    @pl.when(has_low & has_high)
    def _():
        pl.semaphore_wait(barrier, common + 2)

    @pl.when(jnp.logical_not(has_low & has_high))
    def _():
        pl.semaphore_wait(barrier, common + 1)

    lon_copies = []
    for d in (1, lon_parts - 1, 2):
        other = (lon + d) % lon_parts
        copy = pltpu.make_async_remote_copy(
            src_ref=fields.at[:, pl.ds(other * chans, chans), :],
            dst_ref=blocks.at[lon],
            send_sem=sem_lon_s.at[d - 1],
            recv_sem=sem_lon_r.at[d - 1],
            device_id=(lat, other),
            device_id_type=MESH,
        )
        copy.start()
        lon_copies.append((d, copy))

    cells = lax.broadcasted_iota(jnp.int32, (1, 2 * HALF), 1) % HALF
    meta_v[...] = jnp.zeros_like(meta_v)
    meta_r[...] = jnp.zeros_like(meta_r)
    meta_c[...] = jnp.zeros_like(meta_c)
    for at in (0, HALF):
        meta_v[:, at : at + SUPPORT] = values[...]
        meta_r[:, at : at + SUPPORT] = row_off[...]
        meta_c[:, at : at + SUPPORT] = col_off[...]
    get_shift.wait()
    weights_f32 = weights[...].astype(f32)
    shift_row = lax.broadcasted_iota(jnp.int32, (2 * HALF, 2 * HALF), 0)
    shift_lane = lax.broadcasted_iota(jnp.int32, (2 * HALF, 2 * HALF), 1)
    same_half = shift_row // HALF == shift_lane // HALF
    shift_of_row = shift_row % HALF - LON_REACH
    for i in range(lat_dev):
        live = (cells < sizes[i]).astype(f32)
        scaled = meta_v[i : i + 1, :] * live
        effective = (weights_f32 * scaled).astype(bf16).astype(f32)
        rows_of = meta_r[i : i + 1, :]
        for r in range(ROWS):
            left[r * 128 : (r + 1) * 128, :] = jnp.where(
                rows_of == r - LAT_REACH, effective, 0.0
            ).astype(bf16)
        pick = (same_half & (shift_of_row == meta_c[i : i + 1, :])).astype(f32).astype(bf16)
        turns = jnp.dot(shift[...], pick, preferred_element_type=f32).astype(bf16)
        w[i] = lax.dot_general(left[...], turns, NT, preferred_element_type=f32)

    def transform(block):
        data = blocks[block].reshape(lat_dev * chans, blocks.shape[3])
        part = jnp.dot(data, four[block], preferred_element_type=f32)
        return part.reshape(lat_dev, chans, 2 * deg)

    get_own.wait()
    get_four.wait()
    own = pl.ds(LAT_REACH, lat_dev)
    xs[own] = transform(lon)
    for d, copy in lon_copies:
        copy.wait_recv()
        xs[own] += transform((lon + lon_parts - d) % lon_parts)

    up = pltpu.make_async_remote_copy(
        src_ref=xs.at[pl.ds(lat_dev, LAT_REACH)],
        dst_ref=xs.at[pl.ds(0, LAT_REACH)],
        send_sem=sem_halo_s.at[0],
        recv_sem=sem_halo_r.at[0],
        device_id=((lat + 1) % lat_parts, lon),
        device_id_type=MESH,
    )
    down = pltpu.make_async_remote_copy(
        src_ref=xs.at[pl.ds(LAT_REACH, LAT_REACH)],
        dst_ref=xs.at[pl.ds(LAT_REACH + lat_dev, LAT_REACH)],
        send_sem=sem_halo_s.at[1],
        recv_sem=sem_halo_r.at[1],
        device_id=((lat + lat_parts - 1) % lat_parts, lon),
        device_id_type=MESH,
    )

    @pl.when(has_high)
    def _():
        up.start()

    @pl.when(has_low)
    def _():
        down.start()

    @pl.when(jnp.logical_not(has_low))
    def _():
        xs[0:LAT_REACH] = jnp.zeros((LAT_REACH,) + xs.shape[1:], f32)

    @pl.when(jnp.logical_not(has_high))
    def _():
        xs[LAT_REACH + lat_dev :] = jnp.zeros((LAT_REACH,) + xs.shape[1:], f32)

    groups = chans // GROUP

    def products(i, g, o, rows, x_rows):
        real = imag = None
        at = pl.multiple_of(g * (GROUP * GROUP), GROUP * GROUP) + o * GROUP
        for row, (xr, xi) in zip(rows, x_rows):
            tile = w[i, pl.ds(pl.multiple_of((row - i) * 128 + at, GROUP), GROUP), :]
            wr, wi = tile[:, :deg], tile[:, deg:]
            re, im = wr * xr - wi * xi, wr * xi + wi * xr
            real, imag = (re, im) if real is None else (real + re, imag + im)
        return real, imag

    def load_rows(rows, g):
        tiles = [xs[row, pl.ds(pl.multiple_of(g * GROUP, GROUP), GROUP), :] for row in rows]
        return [(t[:, :deg], t[:, deg:]) for t in tiles]

    def own_rows(ig, carry):
        i, g = ig // groups, ig % groups
        rows = [LAT_REACH + j for j in range(lat_dev)]
        x_rows = load_rows(rows, g)
        for o in range(GROUP):
            real, imag = products(i, g, o, rows, x_rows)
            acc[ig, o * GROUP : (o + 1) * GROUP, :deg] = real
            acc[ig, o * GROUP : (o + 1) * GROUP, deg:] = imag
        return carry

    lax.fori_loop(0, lat_dev * groups, own_rows, 0)

    @pl.when(has_low)
    def _():
        up.wait_recv()

    @pl.when(has_high)
    def _():
        down.wait_recv()

    def other_rows(ig, carry):
        i, g = ig // groups, ig % groups
        rows = [i + j + lat_dev * ((i + j) // LAT_REACH) for j in range(LAT_REACH)]
        x_rows = load_rows(rows, g)
        for o in range(GROUP):
            real, imag = products(i, g, o, rows, x_rows)
            real += acc[ig, o * GROUP : (o + 1) * GROUP, :deg]
            imag += acc[ig, o * GROUP : (o + 1) * GROUP, deg:]
            z[ig, 2 * o : 2 * o + 1, :] = jnp.sum(real, axis=0, keepdims=True)
            z[ig, 2 * o + 1 : 2 * o + 2, :] = jnp.sum(imag, axis=0, keepdims=True)
        return carry

    lax.fori_loop(0, lat_dev * groups, other_rows, 0)

    by_order = z[...].reshape(128, deg).T.astype(bf16)
    send_a[...] = by_order.reshape(y_count, 2 * ZC, 128)
    a_copies = []
    for d in range(1, y_count):
        other = (y + d) % y_count
        copy = pltpu.make_async_remote_copy(
            src_ref=send_a.at[other],
            dst_ref=recv_a.at[y],
            send_sem=sem_a_s.at[d - 1],
            recv_sem=sem_a_r.at[d - 1],
            device_id=(other * ZC + zc, lon),
            device_id_type=MESH,
        )
        copy.start()
        a_copies.append(copy)
    recv_a[y] = send_a[y]

    half = lax.broadcasted_iota(jnp.int32, (8, lat_parts), 0) // lat_dev
    orders = (2 * lat + half).astype(f32)
    order_square = orders * orders
    cosine, log_sine, weight = per_lat[0], per_lat[1], per_lat[2]
    norm = jnp.where(half == 0, scalars[2 * deg + 2 * lat], scalars[2 * deg + 2 * lat + 1])
    start = jnp.exp(norm + orders * log_sine)

    def advance(l, state):
        previous, before, inverse, degree = state
        denominator = degree * degree - order_square
        root = lax.rsqrt(jnp.maximum(denominator, 1.0))
        first = jnp.where(denominator > 0.0, scalars[l] * root, 0.0)
        second = first * inverse
        fresh = first * cosine * previous - second * before
        fresh += jnp.where(denominator == 0.0, start, 0.0)
        table[pl.ds(pl.multiple_of(l * 8, 8), 8), :] = fresh * weight
        inverse = jnp.maximum(denominator, 0.0) * root * scalars[deg + l]
        return fresh, previous, inverse, degree + 1.0

    zeros = cosine * 0.0
    lax.fori_loop(0, deg, advance, (zeros, zeros, zeros, zeros), unroll=8)

    for copy in a_copies:
        copy.wait_recv()

    wide_a[...] = recv_a[...].astype(f32).reshape(deg, 128)
    b_copies = []
    for d in range(ZC):
        other = (zc + d) % ZC
        low = wide_a[pl.ds(2 * other, y_count, stride=2 * ZC), :]
        high = wide_a[pl.ds(2 * other + 1, y_count, stride=2 * ZC), :]
        tile = jnp.concatenate([low, high], axis=0).astype(bf16)
        if d == 0:
            recv_b[zc] = tile
            continue
        send_b[other] = tile
        copy = pltpu.make_async_remote_copy(
            src_ref=send_b.at[other],
            dst_ref=recv_b.at[zc],
            send_sem=sem_b_s.at[d - 1],
            recv_sem=sem_b_r.at[d - 1],
            device_id=(y * ZC + other, lon),
            device_id_type=MESH,
        )
        copy.start()
        b_copies.append(copy)

    for s in range(8):
        exact = table[pl.ds(s, deg, stride=8), :]
        high = exact.astype(bf16)
        tcat[s, :, :lat_parts] = high
        tcat[s, :, lat_parts:] = (exact - high.astype(f32)).astype(bf16)

    for copy in b_copies:
        copy.wait_recv()

    arrived = recv_b[...].astype(f32)
    for m in range(2):
        of_order = arrived[:, m * y_count : (m + 1) * y_count, :].reshape(lat_parts, 128)
        by_lat = of_order.T.astype(bf16)
        total = None
        for i in range(lat_dev):
            part = by_lat[i * 32 : (i + 1) * 32, :]
            part = jnp.concatenate([part, part], axis=1)
            term = lax.dot_general(part, tcat[m * lat_dev + i], NT, preferred_element_type=f32)
            total = term if total is None else total + term
        out[:, m * deg : (m + 1) * deg] = total

    for _, copy in lon_copies:
        copy.wait_send()

    @pl.when(has_high)
    def _():
        up.wait_send()

    @pl.when(has_low)
    def _():
        down.wait_send()

    for copy in a_copies + b_copies:
        copy.wait_send()


def body(consts, fields, filter_weights, filter_values, row_offsets, col_offsets, support_sizes):
    _, lat_dev, all_chans, lon_dev = fields.shape
    lat_parts, lon_parts = lax.axis_size("lat"), lax.axis_size("lon")
    chans, deg, y_count = all_chans // lon_parts, 2 * lat_parts, lat_parts // ZC
    own = lax.dynamic_slice_in_dim(filter_weights, lax.axis_index("lon") * chans, chans, 1)
    own = own.transpose(1, 2, 0).reshape(chans * GROUP, SUPPORT)
    own = jnp.pad(own, ((0, 0), (0, HALF - SUPPORT)))
    own = jnp.concatenate([own, own], axis=1)
    vmem, smem = pl.BlockSpec(memory_space=pltpu.VMEM), pl.BlockSpec(memory_space=pltpu.SMEM)
    hbm = pl.BlockSpec(memory_space=pl.ANY)
    f32, bf16, dma = jnp.float32, jnp.bfloat16, pltpu.SemaphoreType.DMA
    result = pl.pallas_call(
        kernel,
        out_shape=jax.ShapeDtypeStruct((chans * 2, 2 * deg), f32),
        in_specs=[hbm, vmem, vmem, vmem, vmem, smem, hbm, hbm, vmem, smem],
        out_specs=vmem,
        scratch_shapes=[
            pltpu.VMEM((lon_parts, lat_dev, chans, lon_dev), bf16),
            pltpu.VMEM((lon_parts, lon_dev, 2 * deg), bf16),
            pltpu.VMEM((2 * deg, 2 * HALF), bf16),
            pltpu.VMEM((lat_dev + 2 * LAT_REACH, chans, 2 * deg), f32),
            pltpu.VMEM((lat_dev, 2 * HALF), f32),
            pltpu.VMEM((lat_dev, 2 * HALF), jnp.int32),
            pltpu.VMEM((lat_dev, 2 * HALF), jnp.int32),
            pltpu.VMEM((ROWS * chans * GROUP, 2 * HALF), bf16),
            pltpu.VMEM((lat_dev, ROWS * chans * GROUP, 2 * deg), f32),
            pltpu.VMEM((lat_dev * chans // GROUP, GROUP * GROUP, 2 * deg), f32),
            pltpu.VMEM((lat_dev * chans // GROUP, 2 * GROUP, deg), f32),
            pltpu.VMEM((y_count, 2 * ZC, 128), bf16),
            pltpu.VMEM((y_count, 2 * ZC, 128), bf16),
            pltpu.VMEM((deg, 128), f32),
            pltpu.VMEM((ZC, 2 * y_count, 128), bf16),
            pltpu.VMEM((ZC, 2 * y_count, 128), bf16),
            pltpu.VMEM((deg * 8, lat_parts), f32),
            pltpu.VMEM((8, deg, 2 * lat_parts), bf16),
            dma((3,)),
            dma((lon_parts - 1,)),
            dma((lon_parts - 1,)),
            dma((2,)),
            dma((2,)),
            dma((y_count - 1,)),
            dma((y_count - 1,)),
            dma((ZC - 1,)),
            dma((ZC - 1,)),
        ],
        compiler_params=pltpu.CompilerParams(
            collective_id=0, has_side_effects=True, vmem_limit_bytes=40 * 1024 * 1024
        ),
    )(
        fields[0], own, filter_values, row_offsets, col_offsets, support_sizes,
        *(jnp.asarray(c) for c in consts),
    )
    return result.reshape(1, chans, 2, 2, deg)


def solution(mesh):
    placed = (
        P(None, "lat", None, "lon"),
        P(),
        P("lat", None),
        P("lat", None),
        P("lat", None),
        P("lat"),
    )

    def whole(fields, *rest):
        lat_parts, lon_parts = mesh.shape["lat"], mesh.shape["lon"]
        consts = tables(
            lat_parts, lon_parts, fields.shape[3] // lon_parts, fields.shape[1] // lat_parts
        )
        return jax.shard_map(
            functools.partial(body, consts),
            mesh=mesh,
            in_specs=placed,
            out_specs=P(None, "lon", None, "lat", None),
            check_vma=False,
        )(fields, *rest)

    return whole
```

```python
import functools
import math

import jax
import jax.numpy as jnp
import ml_dtypes
import numpy as np
from jax import lax
from jax.experimental import pallas as pl
from jax.experimental.pallas import tpu as pltpu
from jax.sharding import PartitionSpec as P

GROUP = 8
SUPPORT = 49
LAT_REACH = 3
LON_REACH = 16
ROWS = 2 * LAT_REACH + 1
HALF = 64
ZC = 16
MESH = pl.DeviceIdType.MESH
NT = (((1,), (1,)), ((), ()))


def split(x):
    high = x.astype(ml_dtypes.bfloat16)
    low = (x - high.astype(np.float64)).astype(ml_dtypes.bfloat16)
    return high, low


def tables(lat_parts, lon_parts, lon_dev, lat_dev):
    nlon, nlat, deg = lon_parts * lon_dev, lat_parts * lat_dev, 2 * lat_parts
    orders = np.arange(deg)
    phase = 2.0 * math.pi / nlon * ((np.arange(nlon)[:, None] * orders[None, :]) % nlon)
    fourier = np.concatenate([np.cos(phase), -np.sin(phase)], 1).astype(ml_dtypes.bfloat16)
    fourier = fourier.reshape(lon_parts, lon_dev, 2 * deg)
    shifts = np.arange(-LON_REACH, LON_REACH + 1)
    turn = 2.0 * math.pi / nlon * ((orders[:, None] * shifts[None, :]) % nlon)
    turn = np.concatenate([np.cos(turn), np.sin(turn)], 0)
    shift_table = np.zeros((2 * deg, 2 * HALF), ml_dtypes.bfloat16)
    shift_table[:, : shifts.size], shift_table[:, HALF : HALF + shifts.size] = split(turn)
    y_count = lat_parts // ZC
    lane = np.arange(lat_parts)
    band = (lane % y_count) * ZC + lane // y_count
    lats = lat_dev * band[None, :] + (np.arange(8) % lat_dev)[:, None]
    colat = math.pi * (lats + 0.5) / nlat
    per_lat = np.stack([np.cos(colat), np.log(np.sin(colat)), math.pi / nlat * np.sin(colat)])
    factors = np.arange(1, deg)
    log_product = np.concatenate([[0.0], np.cumsum(np.log((2.0 * factors - 1) / (2.0 * factors)))])
    log_norm = 0.5 * (np.log((2.0 * orders + 1) / (4 * math.pi)) + log_product)
    grow = np.sqrt(np.maximum(4.0 * orders * orders - 1, 1.0))
    scalars = np.concatenate([grow, 1.0 / grow, log_norm])
    return fourier, shift_table, per_lat.astype(np.float32), scalars.astype(np.float32)


def kernel(
    fields, raw_h, values_h, row_off_h, col_off_h, sizes_h, fourier, shift_table, per_lat_h, scalars_h,
    out,
    raw, values, row_off, col_off, sizes, per_lat, scalars, wide_w, turned, own_turned, weights,
    blocks, four, shift, xs, meta_v, meta_r, meta_c, left, w, acc, z, send_a, recv_a, wide_a, send_b, recv_b,
    table, tcat,
    sem_in, sem_lon_s, sem_lon_r, sem_halo_s, sem_halo_r, sem_a_s, sem_a_r, sem_b_s, sem_b_r,
):
    lat, lon = lax.axis_index("lat"), lax.axis_index("lon")
    lat_parts, lon_parts = lax.axis_size("lat"), lax.axis_size("lon")
    y_count = lat_parts // ZC
    y, zc = lat // ZC, lat % ZC
    lat_dev, chans = blocks.shape[1], blocks.shape[2]
    deg = 2 * lat_parts
    f32, bf16 = jnp.float32, jnp.bfloat16

    barrier = pltpu.get_barrier_semaphore()
    for d in range(1, lon_parts):
        pl.semaphore_signal(barrier, 1, device_id=(lat, (lon + d) % lon_parts), device_id_type=MESH)
    for d in range(1, y_count):
        pl.semaphore_signal(
            barrier, 1, device_id=((y + d) % y_count * ZC + zc, lon), device_id_type=MESH
        )
    for d in range(1, ZC):
        pl.semaphore_signal(barrier, 1, device_id=(y * ZC + (zc + d) % ZC, lon), device_id_type=MESH)
    has_low, has_high = lat > 0, lat < lat_parts - 1

    @pl.when(has_low)
    def _():
        pl.semaphore_signal(barrier, 1, device_id=(lat - 1, lon), device_id_type=MESH)

    @pl.when(has_high)
    def _():
        pl.semaphore_signal(barrier, 1, device_id=(lat + 1, lon), device_id_type=MESH)

    own_block = fields.at[:, pl.ds(lon * chans, chans), :]
    pairs = (
        (raw_h, raw), (values_h, values), (row_off_h, row_off), (col_off_h, col_off),
        (sizes_h, sizes), (shift_table, shift), (own_block, blocks.at[lon]), (fourier, four),
        (per_lat_h, per_lat), (scalars_h, scalars),
    )
    fetches = [pltpu.make_async_copy(p, q, sem_in.at[n]) for n, (p, q) in enumerate(pairs)]
    for fetch in fetches:
        fetch.start()

    common = (lon_parts - 1) + (y_count - 1) + (ZC - 1)

    @pl.when(has_low & has_high)
    def _():
        pl.semaphore_wait(barrier, common + 2)

    @pl.when(jnp.logical_not(has_low & has_high))
    def _():
        pl.semaphore_wait(barrier, common + 1)

    lon_copies = []
    for d in (1, lon_parts - 1, 2):
        other = (lon + d) % lon_parts
        copy = pltpu.make_async_remote_copy(
            src_ref=fields.at[:, pl.ds(other * chans, chans), :],
            dst_ref=blocks.at[lon],
            send_sem=sem_lon_s.at[d - 1],
            recv_sem=sem_lon_r.at[d - 1],
            device_id=(lat, other),
            device_id_type=MESH,
        )
        copy.start()
        lon_copies.append((d, copy))

    for fetch in fetches[:6]:
        fetch.wait()
    cells = lax.broadcasted_iota(jnp.int32, (1, 2 * HALF), 1) % HALF
    meta_v[...] = jnp.zeros_like(meta_v)
    meta_r[...] = jnp.zeros_like(meta_r)
    meta_c[...] = jnp.zeros_like(meta_c)
    for at in (0, HALF):
        meta_v[:, at : at + SUPPORT] = values[...]
        meta_r[:, at : at + SUPPORT] = row_off[...]
        meta_c[:, at : at + SUPPORT] = col_off[...]
    wide_w[...] = jnp.zeros_like(wide_w)
    flat = raw[...].astype(f32).reshape(SUPPORT * GROUP, raw.shape[2])
    for at in (0, HALF * GROUP):
        wide_w[at : at + SUPPORT * GROUP, : raw.shape[2]] = flat
    for a in range(GROUP):
        turned[...] = wide_w[pl.ds(a, 2 * HALF, stride=GROUP), :].T
        own_turned[a * chans : (a + 1) * chans, :] = turned[
            pl.ds(pl.multiple_of(lon * chans, chans), chans), :
        ]
    for o in range(chans):
        weights[o * GROUP : (o + 1) * GROUP, :] = own_turned[pl.ds(o, GROUP, stride=chans), :]
    weights_f32 = weights[...]
    shift_row = lax.broadcasted_iota(jnp.int32, (2 * HALF, 2 * HALF), 0)
    shift_lane = lax.broadcasted_iota(jnp.int32, (2 * HALF, 2 * HALF), 1)
    same_half = shift_row // HALF == shift_lane // HALF
    shift_of_row = shift_row % HALF - LON_REACH
    for i in range(lat_dev):
        live = (cells < sizes[i]).astype(f32)
        scaled = meta_v[i : i + 1, :] * live
        effective = (weights_f32 * scaled).astype(bf16).astype(f32)
        rows_of = meta_r[i : i + 1, :]
        for r in range(ROWS):
            left[r * 128 : (r + 1) * 128, :] = jnp.where(
                rows_of == r - LAT_REACH, effective, 0.0
            ).astype(bf16)
        pick = (same_half & (shift_of_row == meta_c[i : i + 1, :])).astype(f32).astype(bf16)
        turns = jnp.dot(shift[...], pick, preferred_element_type=f32).astype(bf16)
        w[i] = lax.dot_general(left[...], turns, NT, preferred_element_type=f32)

    def transform(block):
        data = blocks[block].reshape(lat_dev * chans, blocks.shape[3])
        part = jnp.dot(data, four[block], preferred_element_type=f32)
        return part.reshape(lat_dev, chans, 2 * deg)

    fetches[6].wait()
    fetches[7].wait()
    own = pl.ds(LAT_REACH, lat_dev)
    xs[own] = transform(lon)
    for d, copy in lon_copies:
        copy.wait_recv()
        xs[own] += transform((lon + lon_parts - d) % lon_parts)

    up = pltpu.make_async_remote_copy(
        src_ref=xs.at[pl.ds(lat_dev, LAT_REACH)],
        dst_ref=xs.at[pl.ds(0, LAT_REACH)],
        send_sem=sem_halo_s.at[0],
        recv_sem=sem_halo_r.at[0],
        device_id=((lat + 1) % lat_parts, lon),
        device_id_type=MESH,
    )
    down = pltpu.make_async_remote_copy(
        src_ref=xs.at[pl.ds(LAT_REACH, LAT_REACH)],
        dst_ref=xs.at[pl.ds(LAT_REACH + lat_dev, LAT_REACH)],
        send_sem=sem_halo_s.at[1],
        recv_sem=sem_halo_r.at[1],
        device_id=((lat + lat_parts - 1) % lat_parts, lon),
        device_id_type=MESH,
    )

    @pl.when(has_high)
    def _():
        up.start()

    @pl.when(has_low)
    def _():
        down.start()

    @pl.when(jnp.logical_not(has_low))
    def _():
        xs[0:LAT_REACH] = jnp.zeros((LAT_REACH,) + xs.shape[1:], f32)

    @pl.when(jnp.logical_not(has_high))
    def _():
        xs[LAT_REACH + lat_dev :] = jnp.zeros((LAT_REACH,) + xs.shape[1:], f32)

    groups = chans // GROUP

    def products(i, g, o, rows, x_rows):
        real = imag = None
        at = pl.multiple_of(g * (GROUP * GROUP), GROUP * GROUP) + o * GROUP
        for row, (xr, xi) in zip(rows, x_rows):
            tile = w[i, pl.ds(pl.multiple_of((row - i) * 128 + at, GROUP), GROUP), :]
            wr, wi = tile[:, :deg], tile[:, deg:]
            re, im = wr * xr - wi * xi, wr * xi + wi * xr
            real, imag = (re, im) if real is None else (real + re, imag + im)
        return real, imag

    def load_rows(rows, g):
        tiles = [xs[row, pl.ds(pl.multiple_of(g * GROUP, GROUP), GROUP), :] for row in rows]
        return [(t[:, :deg], t[:, deg:]) for t in tiles]

    def own_rows(ig, carry):
        i, g = ig // groups, ig % groups
        rows = [LAT_REACH + j for j in range(lat_dev)]
        x_rows = load_rows(rows, g)
        for o in range(GROUP):
            real, imag = products(i, g, o, rows, x_rows)
            acc[ig, o * GROUP : (o + 1) * GROUP, :deg] = real
            acc[ig, o * GROUP : (o + 1) * GROUP, deg:] = imag
        return carry

    lax.fori_loop(0, lat_dev * groups, own_rows, 0)

    @pl.when(has_low)
    def _():
        up.wait_recv()

    @pl.when(has_high)
    def _():
        down.wait_recv()

    def other_rows(ig, carry):
        i, g = ig // groups, ig % groups
        rows = [i + j + lat_dev * ((i + j) // LAT_REACH) for j in range(LAT_REACH)]
        x_rows = load_rows(rows, g)
        for o in range(GROUP):
            real, imag = products(i, g, o, rows, x_rows)
            real += acc[ig, o * GROUP : (o + 1) * GROUP, :deg]
            imag += acc[ig, o * GROUP : (o + 1) * GROUP, deg:]
            z[ig, 2 * o : 2 * o + 1, :] = jnp.sum(real, axis=0, keepdims=True)
            z[ig, 2 * o + 1 : 2 * o + 2, :] = jnp.sum(imag, axis=0, keepdims=True)
        return carry

    lax.fori_loop(0, lat_dev * groups, other_rows, 0)

    by_order = z[...].reshape(128, deg).T.astype(bf16)
    send_a[...] = by_order.reshape(y_count, 2 * ZC, 128)
    a_copies = []
    for d in range(1, y_count):
        other = (y + d) % y_count
        copy = pltpu.make_async_remote_copy(
            src_ref=send_a.at[other],
            dst_ref=recv_a.at[y],
            send_sem=sem_a_s.at[d - 1],
            recv_sem=sem_a_r.at[d - 1],
            device_id=(other * ZC + zc, lon),
            device_id_type=MESH,
        )
        copy.start()
        a_copies.append(copy)
    recv_a[y] = send_a[y]

    fetches[8].wait()
    fetches[9].wait()
    half = lax.broadcasted_iota(jnp.int32, (8, lat_parts), 0) // lat_dev
    orders = (2 * lat + half).astype(f32)
    order_square = orders * orders
    cosine, log_sine, weight = per_lat[0], per_lat[1], per_lat[2]
    norm = jnp.where(half == 0, scalars[2 * deg + 2 * lat], scalars[2 * deg + 2 * lat + 1])
    start = jnp.exp(norm + orders * log_sine)

    def advance(l, state):
        previous, before, inverse, degree = state
        denominator = degree * degree - order_square
        root = lax.rsqrt(jnp.maximum(denominator, 1.0))
        first = jnp.where(denominator > 0.0, scalars[l] * root, 0.0)
        second = first * inverse
        fresh = first * cosine * previous - second * before
        fresh += jnp.where(denominator == 0.0, start, 0.0)
        table[pl.ds(pl.multiple_of(l * 8, 8), 8), :] = fresh * weight
        inverse = jnp.maximum(denominator, 0.0) * root * scalars[deg + l]
        return fresh, previous, inverse, degree + 1.0

    zeros = cosine * 0.0
    lax.fori_loop(0, deg, advance, (zeros, zeros, zeros, zeros), unroll=8)

    for copy in a_copies:
        copy.wait_recv()

    wide_a[...] = recv_a[...].astype(f32).reshape(deg, 128)
    b_copies = []
    for d in range(ZC):
        other = (zc + d) % ZC
        low = wide_a[pl.ds(2 * other, y_count, stride=2 * ZC), :]
        high = wide_a[pl.ds(2 * other + 1, y_count, stride=2 * ZC), :]
        tile = jnp.concatenate([low, high], axis=0).astype(bf16)
        if d == 0:
            recv_b[zc] = tile
            continue
        send_b[other] = tile
        copy = pltpu.make_async_remote_copy(
            src_ref=send_b.at[other],
            dst_ref=recv_b.at[zc],
            send_sem=sem_b_s.at[d - 1],
            recv_sem=sem_b_r.at[d - 1],
            device_id=(y * ZC + other, lon),
            device_id_type=MESH,
        )
        copy.start()
        b_copies.append(copy)

    for s in range(8):
        exact = table[pl.ds(s, deg, stride=8), :]
        high = exact.astype(bf16)
        tcat[s, :, :lat_parts] = high
        tcat[s, :, lat_parts:] = (exact - high.astype(f32)).astype(bf16)

    for copy in b_copies:
        copy.wait_recv()

    arrived = recv_b[...].astype(f32)
    for m in range(2):
        of_order = arrived[:, m * y_count : (m + 1) * y_count, :].reshape(lat_parts, 128)
        by_lat = of_order.T.astype(bf16)
        total = None
        for i in range(lat_dev):
            part = by_lat[i * 32 : (i + 1) * 32, :]
            part = jnp.concatenate([part, part], axis=1)
            term = lax.dot_general(part, tcat[m * lat_dev + i], NT, preferred_element_type=f32)
            total = term if total is None else total + term
        out[:, m * deg : (m + 1) * deg] = total

    for _, copy in lon_copies:
        copy.wait_send()

    @pl.when(has_high)
    def _():
        up.wait_send()

    @pl.when(has_low)
    def _():
        down.wait_send()

    for copy in a_copies + b_copies:
        copy.wait_send()


def body(consts, fields, filter_weights, filter_values, row_offsets, col_offsets, support_sizes):
    _, lat_dev, all_chans, lon_dev = fields.shape
    lat_parts, lon_parts = lax.axis_size("lat"), lax.axis_size("lon")
    chans, deg, y_count = all_chans // lon_parts, 2 * lat_parts, lat_parts // ZC
    vmem, hbm = pl.BlockSpec(memory_space=pltpu.VMEM), pl.BlockSpec(memory_space=pltpu.HBM)
    f32, bf16, dma = jnp.float32, jnp.bfloat16, pltpu.SemaphoreType.DMA
    result = pl.pallas_call(
        kernel,
        out_shape=jax.ShapeDtypeStruct((chans * 2, 2 * deg), f32),
        in_specs=[hbm] * 10,
        out_specs=vmem,
        scratch_shapes=[
            pltpu.VMEM((SUPPORT, GROUP, all_chans), bf16),
            pltpu.VMEM((lat_dev, SUPPORT), f32),
            pltpu.VMEM((lat_dev, SUPPORT), jnp.int32),
            pltpu.VMEM((lat_dev, SUPPORT), jnp.int32),
            pltpu.SMEM((lat_dev,), jnp.int32),
            pltpu.VMEM((3, 8, lat_parts), f32),
            pltpu.SMEM((3 * deg,), f32),
            pltpu.VMEM((2 * HALF * GROUP, 128), f32),
            pltpu.VMEM((128, 2 * HALF), f32),
            pltpu.VMEM((chans * GROUP, 2 * HALF), f32),
            pltpu.VMEM((chans * GROUP, 2 * HALF), f32),
            pltpu.VMEM((lon_parts, lat_dev, chans, lon_dev), bf16),
            pltpu.VMEM((lon_parts, lon_dev, 2 * deg), bf16),
            pltpu.VMEM((2 * deg, 2 * HALF), bf16),
            pltpu.VMEM((lat_dev + 2 * LAT_REACH, chans, 2 * deg), f32),
            pltpu.VMEM((lat_dev, 2 * HALF), f32),
            pltpu.VMEM((lat_dev, 2 * HALF), jnp.int32),
            pltpu.VMEM((lat_dev, 2 * HALF), jnp.int32),
            pltpu.VMEM((ROWS * chans * GROUP, 2 * HALF), bf16),
            pltpu.VMEM((lat_dev, ROWS * chans * GROUP, 2 * deg), f32),
            pltpu.VMEM((lat_dev * chans // GROUP, GROUP * GROUP, 2 * deg), f32),
            pltpu.VMEM((lat_dev * chans // GROUP, 2 * GROUP, deg), f32),
            pltpu.VMEM((y_count, 2 * ZC, 128), bf16),
            pltpu.VMEM((y_count, 2 * ZC, 128), bf16),
            pltpu.VMEM((deg, 128), f32),
            pltpu.VMEM((ZC, 2 * y_count, 128), bf16),
            pltpu.VMEM((ZC, 2 * y_count, 128), bf16),
            pltpu.VMEM((deg * 8, lat_parts), f32),
            pltpu.VMEM((8, deg, 2 * lat_parts), bf16),
            dma((10,)),
            dma((lon_parts - 1,)),
            dma((lon_parts - 1,)),
            dma((2,)),
            dma((2,)),
            dma((y_count - 1,)),
            dma((y_count - 1,)),
            dma((ZC - 1,)),
            dma((ZC - 1,)),
        ],
        compiler_params=pltpu.CompilerParams(
            collective_id=0, has_side_effects=True, vmem_limit_bytes=60 * 1024 * 1024
        ),
    )(
        fields[0], filter_weights.transpose(0, 2, 1), filter_values, row_offsets, col_offsets, support_sizes,
        *(jnp.asarray(c) for c in consts),
    )
    return result.reshape(1, chans, 2, 2, deg)


def solution(mesh):
    placed = (
        P(None, "lat", None, "lon"),
        P(),
        P("lat", None),
        P("lat", None),
        P("lat", None),
        P("lat"),
    )

    def whole(fields, *rest):
        lat_parts, lon_parts = mesh.shape["lat"], mesh.shape["lon"]
        consts = tables(
            lat_parts, lon_parts, fields.shape[3] // lon_parts, fields.shape[1] // lat_parts
        )
        return jax.shard_map(
            functools.partial(body, consts),
            mesh=mesh,
            in_specs=placed,
            out_specs=P(None, "lon", None, "lat", None),
            check_vma=False,
        )(fields, *rest)

    return whole
```

```python
import functools
import math

import jax
import jax.numpy as jnp
import ml_dtypes
import numpy as np
from jax import lax
from jax.experimental import pallas as pl
from jax.experimental.pallas import tpu as pltpu
from jax.sharding import PartitionSpec as P

GROUP = 8
SUPPORT = 49
LAT_REACH = 3
LON_REACH = 16
ROWS = 2 * LAT_REACH + 1
HALF = 64
ZC = 16
MESH = pl.DeviceIdType.MESH
NT = (((1,), (1,)), ((), ()))


def split(x):
    high = x.astype(ml_dtypes.bfloat16)
    low = (x - high.astype(np.float64)).astype(ml_dtypes.bfloat16)
    return high, low


def tables(lat_parts, lon_parts, lon_dev, lat_dev):
    nlon, nlat, deg = lon_parts * lon_dev, lat_parts * lat_dev, 2 * lat_parts
    orders = np.arange(deg)
    phase = 2.0 * math.pi / nlon * ((np.arange(nlon)[:, None] * orders[None, :]) % nlon)
    fourier = np.concatenate([np.cos(phase), -np.sin(phase)], 1).astype(ml_dtypes.bfloat16)
    fourier = fourier.reshape(lon_parts, lon_dev, 2 * deg)
    shifts = np.arange(-LON_REACH, LON_REACH + 1)
    turn = 2.0 * math.pi / nlon * ((orders[:, None] * shifts[None, :]) % nlon)
    turn = np.concatenate([np.cos(turn), np.sin(turn)], 0)
    shift_table = np.zeros((2 * deg, 2 * HALF), ml_dtypes.bfloat16)
    shift_table[:, : shifts.size], shift_table[:, HALF : HALF + shifts.size] = split(turn)
    y_count = lat_parts // ZC
    lane = np.arange(lat_parts)
    band = (lane % y_count) * ZC + lane // y_count
    lats = lat_dev * band[None, :] + (np.arange(8) % lat_dev)[:, None]
    colat = math.pi * (lats + 0.5) / nlat
    per_lat = np.stack([np.cos(colat), np.log(np.sin(colat)), math.pi / nlat * np.sin(colat)])
    factors = np.arange(1, deg)
    log_product = np.concatenate([[0.0], np.cumsum(np.log((2.0 * factors - 1) / (2.0 * factors)))])
    log_norm = 0.5 * (np.log((2.0 * orders + 1) / (4 * math.pi)) + log_product)
    grow = np.sqrt(np.maximum(4.0 * orders * orders - 1, 1.0))
    scalars = np.concatenate([grow, 1.0 / grow, log_norm])
    return fourier, shift_table, per_lat.astype(np.float32), scalars.astype(np.float32)


def kernel(
    fields, raw_h, values_h, row_off_h, col_off_h, sizes_h, fourier, shift_table, per_lat_h, scalars_h,
    out,
    raw, values, row_off, col_off, sizes, per_lat, scalars, wide_w, turned, own_turned, weights,
    blocks, four, shift, xs, meta_v, meta_r, meta_c, left, w, acc, z, send_a, recv_a, wide_a, send_b, recv_b,
    table, tcat,
    near, far, sem_in, sem_lon_s, sem_lon_r, sem_halo_s, sem_halo_r, sem_a_s, sem_a_r, sem_b_s, sem_b_r,
):
    lat, lon = lax.axis_index("lat"), lax.axis_index("lon")
    lat_parts, lon_parts = lax.axis_size("lat"), lax.axis_size("lon")
    y_count = lat_parts // ZC
    y, zc = lat // ZC, lat % ZC
    lat_dev, chans = blocks.shape[1], blocks.shape[2]
    deg = 2 * lat_parts
    f32, bf16 = jnp.float32, jnp.bfloat16

    core, z_at = lat % 2, lat // 2 % (ZC // 2)
    z_count = ZC // 2
    barrier = pltpu.get_barrier_semaphore()
    is_low, is_high = core == 0, core == 1
    has_low, has_high = lat > 0, lat < lat_parts - 1
    at_end = (lat < lat_parts - 2) & (z_at == z_count - 1)
    has_before = (lat > 1) & (z_at == 0)

    def tell(sem, to_lat, to_lon):
        pl.semaphore_signal(sem, 1, device_id=(to_lat, to_lon), device_id_type=MESH)

    for d in range(1, lon_parts):
        tell(barrier, lat - core, (lon + d) % lon_parts)

    @pl.when(is_high)
    def _():
        tell(barrier, lat - 1, lon)

    for d in range(1, y_count):
        tell(barrier, ((y + d) % y_count * z_count + z_at) * 2 + 1, lon)
    for d in range(1, z_count):
        tell(barrier, (y * z_count + (z_at + d) % z_count) * 2 + 1, lon)

    @pl.when(has_before)
    def _():
        tell(barrier, lat - core - 1, lon)

    @pl.when(at_end)
    def _():
        tell(barrier, lat - core + 3, lon)

    own_block = fields.at[:, pl.ds(lon * chans, chans), :]
    pairs = (
        (raw_h, raw), (values_h, values), (row_off_h, row_off), (col_off_h, col_off),
        (sizes_h, sizes), (shift_table, shift), (own_block, blocks.at[lon]), (fourier, four),
        (per_lat_h, per_lat), (scalars_h, scalars),
    )
    fetches = [pltpu.make_async_copy(p, q, sem_in.at[n]) for n, (p, q) in enumerate(pairs)]
    for fetch in fetches:
        fetch.start()

    @pl.when(is_low)
    def _():
        pl.semaphore_wait(barrier, 2 * (lon_parts - 1) + 1)
        tell(near, lat + 1, lon)

    @pl.when(is_high)
    def _():
        pl.semaphore_wait(near, 1)

    lon_copies = []
    for d in (1, lon_parts - 1, 2):
        other = (lon + d) % lon_parts
        copy = pltpu.make_async_remote_copy(
            src_ref=fields.at[:, pl.ds(other * chans, chans), :],
            dst_ref=blocks.at[lon],
            send_sem=sem_lon_s.at[d - 1],
            recv_sem=sem_lon_r.at[d - 1],
            device_id=(lat, other),
            device_id_type=MESH,
        )
        copy.start()
        lon_copies.append((d, copy))

    for fetch in fetches[:6]:
        fetch.wait()
    cells = lax.broadcasted_iota(jnp.int32, (1, 2 * HALF), 1) % HALF
    meta_v[...] = jnp.zeros_like(meta_v)
    meta_r[...] = jnp.zeros_like(meta_r)
    meta_c[...] = jnp.zeros_like(meta_c)
    for at in (0, HALF):
        meta_v[:, at : at + SUPPORT] = values[...]
        meta_r[:, at : at + SUPPORT] = row_off[...]
        meta_c[:, at : at + SUPPORT] = col_off[...]
    wide_w[...] = jnp.zeros_like(wide_w)
    flat = raw[...].astype(f32).reshape(SUPPORT * GROUP, raw.shape[2])
    for at in (0, HALF * GROUP):
        wide_w[at : at + SUPPORT * GROUP, : raw.shape[2]] = flat
    for a in range(GROUP):
        turned[...] = wide_w[pl.ds(a, 2 * HALF, stride=GROUP), :].T
        own_turned[a * chans : (a + 1) * chans, :] = turned[
            pl.ds(pl.multiple_of(lon * chans, chans), chans), :
        ]
    for o in range(chans):
        weights[o * GROUP : (o + 1) * GROUP, :] = own_turned[pl.ds(o, GROUP, stride=chans), :]
    weights_f32 = weights[...]
    shift_row = lax.broadcasted_iota(jnp.int32, (2 * HALF, 2 * HALF), 0)
    shift_lane = lax.broadcasted_iota(jnp.int32, (2 * HALF, 2 * HALF), 1)
    same_half = shift_row // HALF == shift_lane // HALF
    shift_of_row = shift_row % HALF - LON_REACH
    for i in range(lat_dev):
        live = (cells < sizes[i]).astype(f32)
        scaled = meta_v[i : i + 1, :] * live
        effective = (weights_f32 * scaled).astype(bf16).astype(f32)
        rows_of = meta_r[i : i + 1, :]
        for r in range(ROWS):
            left[r * 128 : (r + 1) * 128, :] = jnp.where(
                rows_of == r - LAT_REACH, effective, 0.0
            ).astype(bf16)
        pick = (same_half & (shift_of_row == meta_c[i : i + 1, :])).astype(f32).astype(bf16)
        turns = jnp.dot(shift[...], pick, preferred_element_type=f32).astype(bf16)
        w[i] = lax.dot_general(left[...], turns, NT, preferred_element_type=f32)

    def transform(block):
        data = blocks[block].reshape(lat_dev * chans, blocks.shape[3])
        part = jnp.dot(data, four[block], preferred_element_type=f32)
        return part.reshape(lat_dev, chans, 2 * deg)

    fetches[6].wait()
    fetches[7].wait()
    own = pl.ds(LAT_REACH, lat_dev)
    xs[own] = transform(lon)
    for d, copy in lon_copies:
        copy.wait_recv()
        xs[own] += transform((lon + lon_parts - d) % lon_parts)

    up = pltpu.make_async_remote_copy(
        src_ref=xs.at[pl.ds(lat_dev, LAT_REACH)],
        dst_ref=xs.at[pl.ds(0, LAT_REACH)],
        send_sem=sem_halo_s.at[0],
        recv_sem=sem_halo_r.at[0],
        device_id=((lat + 1) % lat_parts, lon),
        device_id_type=MESH,
    )
    down = pltpu.make_async_remote_copy(
        src_ref=xs.at[pl.ds(LAT_REACH, LAT_REACH)],
        dst_ref=xs.at[pl.ds(LAT_REACH + lat_dev, LAT_REACH)],
        send_sem=sem_halo_s.at[1],
        recv_sem=sem_halo_r.at[1],
        device_id=((lat + lat_parts - 1) % lat_parts, lon),
        device_id_type=MESH,
    )

    @pl.when(is_high)
    def _():
        far_count = 2 * (y_count - 1 + z_count - 1)
        pl.semaphore_wait(barrier, far_count + 2 * (has_before.astype(jnp.int32) + at_end.astype(jnp.int32)))
        tell(far, lat - 1, lon)

    @pl.when(is_low)
    def _():
        pl.semaphore_wait(far, 1)

    @pl.when(has_high)
    def _():
        up.start()

    @pl.when(has_low)
    def _():
        down.start()

    @pl.when(jnp.logical_not(has_low))
    def _():
        xs[0:LAT_REACH] = jnp.zeros((LAT_REACH,) + xs.shape[1:], f32)

    @pl.when(jnp.logical_not(has_high))
    def _():
        xs[LAT_REACH + lat_dev :] = jnp.zeros((LAT_REACH,) + xs.shape[1:], f32)

    groups = chans // GROUP

    def products(i, g, o, rows, x_rows):
        real = imag = None
        at = pl.multiple_of(g * (GROUP * GROUP), GROUP * GROUP) + o * GROUP
        for row, (xr, xi) in zip(rows, x_rows):
            tile = w[i, pl.ds(pl.multiple_of((row - i) * 128 + at, GROUP), GROUP), :]
            wr, wi = tile[:, :deg], tile[:, deg:]
            re, im = wr * xr - wi * xi, wr * xi + wi * xr
            real, imag = (re, im) if real is None else (real + re, imag + im)
        return real, imag

    def load_rows(rows, g):
        tiles = [xs[row, pl.ds(pl.multiple_of(g * GROUP, GROUP), GROUP), :] for row in rows]
        return [(t[:, :deg], t[:, deg:]) for t in tiles]

    def own_rows(ig, carry):
        i, g = ig // groups, ig % groups
        rows = [LAT_REACH + j for j in range(lat_dev)]
        x_rows = load_rows(rows, g)
        for o in range(GROUP):
            real, imag = products(i, g, o, rows, x_rows)
            acc[ig, o * GROUP : (o + 1) * GROUP, :deg] = real
            acc[ig, o * GROUP : (o + 1) * GROUP, deg:] = imag
        return carry

    lax.fori_loop(0, lat_dev * groups, own_rows, 0)

    @pl.when(has_low)
    def _():
        up.wait_recv()

    @pl.when(has_high)
    def _():
        down.wait_recv()

    def other_rows(ig, carry):
        i, g = ig // groups, ig % groups
        rows = [i + j + lat_dev * ((i + j) // LAT_REACH) for j in range(LAT_REACH)]
        x_rows = load_rows(rows, g)
        for o in range(GROUP):
            real, imag = products(i, g, o, rows, x_rows)
            real += acc[ig, o * GROUP : (o + 1) * GROUP, :deg]
            imag += acc[ig, o * GROUP : (o + 1) * GROUP, deg:]
            z[ig, 2 * o : 2 * o + 1, :] = jnp.sum(real, axis=0, keepdims=True)
            z[ig, 2 * o + 1 : 2 * o + 2, :] = jnp.sum(imag, axis=0, keepdims=True)
        return carry

    lax.fori_loop(0, lat_dev * groups, other_rows, 0)

    @pl.when(has_high)
    def _():
        up.wait_send()

    @pl.when(has_low)
    def _():
        down.wait_send()

    by_order = z[...].reshape(128, deg).T.astype(bf16)
    send_a[...] = by_order.reshape(y_count, 2 * ZC, 128)
    a_copies = []
    for d in range(1, y_count):
        other = (y + d) % y_count
        copy = pltpu.make_async_remote_copy(
            src_ref=send_a.at[other],
            dst_ref=recv_a.at[y],
            send_sem=sem_a_s.at[d - 1],
            recv_sem=sem_a_r.at[d - 1],
            device_id=(other * ZC + zc, lon),
            device_id_type=MESH,
        )
        copy.start()
        a_copies.append(copy)
    recv_a[y] = send_a[y]

    fetches[8].wait()
    fetches[9].wait()
    half = lax.broadcasted_iota(jnp.int32, (8, lat_parts), 0) // lat_dev
    orders = (2 * lat + half).astype(f32)
    order_square = orders * orders
    cosine, log_sine, weight = per_lat[0], per_lat[1], per_lat[2]
    norm = jnp.where(half == 0, scalars[2 * deg + 2 * lat], scalars[2 * deg + 2 * lat + 1])
    start = jnp.exp(norm + orders * log_sine)

    def advance(l, state):
        previous, before, inverse, degree = state
        denominator = degree * degree - order_square
        root = lax.rsqrt(jnp.maximum(denominator, 1.0))
        first = jnp.where(denominator > 0.0, scalars[l] * root, 0.0)
        second = first * inverse
        fresh = first * cosine * previous - second * before
        fresh += jnp.where(denominator == 0.0, start, 0.0)
        table[pl.ds(pl.multiple_of(l * 8, 8), 8), :] = fresh * weight
        inverse = jnp.maximum(denominator, 0.0) * root * scalars[deg + l]
        return fresh, previous, inverse, degree + 1.0

    zeros = cosine * 0.0
    lax.fori_loop(0, deg, advance, (zeros, zeros, zeros, zeros), unroll=8)

    for copy in a_copies:
        copy.wait_recv()

    wide_a[...] = recv_a[...].astype(f32).reshape(deg, 128)
    b_copies = []
    for d in range(ZC):
        other = (zc + d) % ZC
        low = wide_a[pl.ds(2 * other, y_count, stride=2 * ZC), :]
        high = wide_a[pl.ds(2 * other + 1, y_count, stride=2 * ZC), :]
        tile = jnp.concatenate([low, high], axis=0).astype(bf16)
        if d == 0:
            recv_b[zc] = tile
            continue
        send_b[other] = tile
        copy = pltpu.make_async_remote_copy(
            src_ref=send_b.at[other],
            dst_ref=recv_b.at[zc],
            send_sem=sem_b_s.at[d - 1],
            recv_sem=sem_b_r.at[d - 1],
            device_id=(y * ZC + other, lon),
            device_id_type=MESH,
        )
        copy.start()
        b_copies.append(copy)

    for s in range(8):
        exact = table[pl.ds(s, deg, stride=8), :]
        high = exact.astype(bf16)
        tcat[s, :, :lat_parts] = high
        tcat[s, :, lat_parts:] = (exact - high.astype(f32)).astype(bf16)

    for copy in b_copies:
        copy.wait_recv()

    arrived = recv_b[...].astype(f32)
    for m in range(2):
        of_order = arrived[:, m * y_count : (m + 1) * y_count, :].reshape(lat_parts, 128)
        by_lat = of_order.T.astype(bf16)
        total = None
        for i in range(lat_dev):
            part = by_lat[i * 32 : (i + 1) * 32, :]
            part = jnp.concatenate([part, part], axis=1)
            term = lax.dot_general(part, tcat[m * lat_dev + i], NT, preferred_element_type=f32)
            total = term if total is None else total + term
        out[0, :, :, m, :] = total.reshape(chans, 2, deg)

    for _, copy in lon_copies:
        copy.wait_send()

    for copy in a_copies + b_copies:
        copy.wait_send()


def body(consts, fields, filter_weights, filter_values, row_offsets, col_offsets, support_sizes):
    _, lat_dev, all_chans, lon_dev = fields.shape
    lat_parts, lon_parts = lax.axis_size("lat"), lax.axis_size("lon")
    chans, deg, y_count = all_chans // lon_parts, 2 * lat_parts, lat_parts // ZC
    vmem, hbm = pl.BlockSpec(memory_space=pltpu.VMEM), pl.BlockSpec(memory_space=pltpu.HBM)
    f32, bf16, dma = jnp.float32, jnp.bfloat16, pltpu.SemaphoreType.DMA
    return pl.pallas_call(
        kernel,
        out_shape=jax.ShapeDtypeStruct((1, chans, 2, 2, deg), f32),
        in_specs=[hbm] * 10,
        out_specs=vmem,
        scratch_shapes=[
            pltpu.VMEM((SUPPORT, GROUP, all_chans), bf16),
            pltpu.VMEM((lat_dev, SUPPORT), f32),
            pltpu.VMEM((lat_dev, SUPPORT), jnp.int32),
            pltpu.VMEM((lat_dev, SUPPORT), jnp.int32),
            pltpu.SMEM((lat_dev,), jnp.int32),
            pltpu.VMEM((3, 8, lat_parts), f32),
            pltpu.SMEM((3 * deg,), f32),
            pltpu.VMEM((2 * HALF * GROUP, 128), f32),
            pltpu.VMEM((128, 2 * HALF), f32),
            pltpu.VMEM((chans * GROUP, 2 * HALF), f32),
            pltpu.VMEM((chans * GROUP, 2 * HALF), f32),
            pltpu.VMEM((lon_parts, lat_dev, chans, lon_dev), bf16),
            pltpu.VMEM((lon_parts, lon_dev, 2 * deg), bf16),
            pltpu.VMEM((2 * deg, 2 * HALF), bf16),
            pltpu.VMEM((lat_dev + 2 * LAT_REACH, chans, 2 * deg), f32),
            pltpu.VMEM((lat_dev, 2 * HALF), f32),
            pltpu.VMEM((lat_dev, 2 * HALF), jnp.int32),
            pltpu.VMEM((lat_dev, 2 * HALF), jnp.int32),
            pltpu.VMEM((ROWS * chans * GROUP, 2 * HALF), bf16),
            pltpu.VMEM((lat_dev, ROWS * chans * GROUP, 2 * deg), f32),
            pltpu.VMEM((lat_dev * chans // GROUP, GROUP * GROUP, 2 * deg), f32),
            pltpu.VMEM((lat_dev * chans // GROUP, 2 * GROUP, deg), f32),
            pltpu.VMEM((y_count, 2 * ZC, 128), bf16),
            pltpu.VMEM((y_count, 2 * ZC, 128), bf16),
            pltpu.VMEM((deg, 128), f32),
            pltpu.VMEM((ZC, 2 * y_count, 128), bf16),
            pltpu.VMEM((ZC, 2 * y_count, 128), bf16),
            pltpu.VMEM((deg * 8, lat_parts), f32),
            pltpu.VMEM((8, deg, 2 * lat_parts), bf16),
            pltpu.SemaphoreType.REGULAR,
            pltpu.SemaphoreType.REGULAR,
            dma((10,)),
            dma((lon_parts - 1,)),
            dma((lon_parts - 1,)),
            dma((2,)),
            dma((2,)),
            dma((y_count - 1,)),
            dma((y_count - 1,)),
            dma((ZC - 1,)),
            dma((ZC - 1,)),
        ],
        compiler_params=pltpu.CompilerParams(
            collective_id=0, has_side_effects=True, vmem_limit_bytes=60 * 1024 * 1024
        ),
    )(
        fields[0], filter_weights.transpose(0, 2, 1), filter_values, row_offsets, col_offsets, support_sizes,
        *(jnp.asarray(c) for c in consts),
    )


def solution(mesh):
    placed = (
        P(None, "lat", None, "lon"),
        P(),
        P("lat", None),
        P("lat", None),
        P("lat", None),
        P("lat"),
    )

    def whole(fields, *rest):
        lat_parts, lon_parts = mesh.shape["lat"], mesh.shape["lon"]
        consts = tables(
            lat_parts, lon_parts, fields.shape[3] // lon_parts, fields.shape[1] // lat_parts
        )
        return jax.shard_map(
            functools.partial(body, consts),
            mesh=mesh,
            in_specs=placed,
            out_specs=P(None, "lon", None, "lat", None),
            check_vma=False,
        )(fields, *rest)

    return whole
```

```python
import functools
import math

import jax
import jax.numpy as jnp
import ml_dtypes
import numpy as np
from jax import lax
from jax.experimental import pallas as pl
from jax.experimental.pallas import tpu as pltpu
from jax.sharding import PartitionSpec as P

GROUP = 8
SUPPORT = 49
LAT_REACH = 3
LON_REACH = 16
ROWS = 2 * LAT_REACH + 1
HALF = 64
Z = 8
MESH = pl.DeviceIdType.MESH
NT = (((1,), (1,)), ((), ()))


def split(x):
    high = x.astype(ml_dtypes.bfloat16)
    low = (x - high.astype(np.float64)).astype(ml_dtypes.bfloat16)
    return high, low


def tables(lat_parts, lon_parts, lon_dev, lat_dev):
    nlon, nlat, deg = lon_parts * lon_dev, lat_parts * lat_dev, 2 * lat_parts
    orders = np.arange(deg)
    phase = 2.0 * math.pi / nlon * ((np.arange(nlon)[:, None] * orders[None, :]) % nlon)
    fourier = np.concatenate([np.cos(phase), -np.sin(phase)], 1).astype(ml_dtypes.bfloat16)
    fourier = fourier.reshape(lon_parts, lon_dev, 2 * deg)
    shifts = np.arange(-LON_REACH, LON_REACH + 1)
    turn = 2.0 * math.pi / nlon * ((orders[:, None] * shifts[None, :]) % nlon)
    turn = np.concatenate([np.cos(turn), np.sin(turn)], 0)
    shift_table = np.zeros((2 * deg, 2 * HALF), ml_dtypes.bfloat16)
    shift_table[:, : shifts.size], shift_table[:, HALF : HALF + shifts.size] = split(turn)
    lane, chips = np.arange(lat_parts), lat_parts // 2
    band = (lane % chips) * 2 + lane // chips
    lats = lat_dev * band[None, :] + (np.arange(8) % lat_dev)[:, None]
    colat = math.pi * (lats + 0.5) / nlat
    per_lat = np.stack([np.cos(colat), np.log(np.sin(colat)), math.pi / nlat * np.sin(colat)])
    factors = np.arange(1, deg)
    log_product = np.concatenate([[0.0], np.cumsum(np.log((2.0 * factors - 1) / (2.0 * factors)))])
    log_norm = 0.5 * (np.log((2.0 * orders + 1) / (4 * math.pi)) + log_product)
    grow = np.sqrt(np.maximum(4.0 * orders * orders - 1, 1.0))
    scalars = np.concatenate([grow, 1.0 / grow, log_norm])
    return fourier, shift_table, per_lat.astype(np.float32), scalars.astype(np.float32)


def kernel(
    fields, raw_h, values_h, row_off_h, col_off_h, sizes_h, fourier, shift_table, per_lat_h, scalars_h,
    out,
    raw, values, row_off, col_off, sizes, per_lat, scalars, wide_w, turned, own_turned, weights,
    blocks, four, shift, xs, meta_v, meta_r, meta_c, left, w, acc, z, send_a, recv_a, wide_a, send_b, recv_b,
    table, tcat,
    near, far, sem_in, sem_lon_s, sem_lon_r, sem_halo_s, sem_halo_r, sem_a_s, sem_a_r, sem_b_s, sem_b_r,
):
    lat, lon = lax.axis_index("lat"), lax.axis_index("lon")
    lat_parts, lon_parts = lax.axis_size("lat"), lax.axis_size("lon")
    chips, y_count = lat_parts // 2, lat_parts // (2 * Z)
    chip, core = lat // 2, lat % 2
    y, z_at = chip // Z, chip % Z
    lat_dev, chans = blocks.shape[1], blocks.shape[2]
    deg = 2 * lat_parts
    f32, bf16 = jnp.float32, jnp.bfloat16

    barrier = pltpu.get_barrier_semaphore()
    is_low, is_high = core == 0, core == 1
    has_low, has_high = lat > 0, lat < lat_parts - 1

    def tell(sem, to_lat, to_lon):
        pl.semaphore_signal(sem, 1, device_id=(to_lat, to_lon), device_id_type=MESH)

    def far_chip(dy, dz):
        return (y + dy) % y_count * Z + (z_at + dz) % Z

    def hops(dy, dz):
        return min(dy, y_count - dy) + min(dz, Z - dz)

    turns = [(dy, dz) for dy in range(y_count) for dz in range(Z) if dy or dz]
    turns.sort(key=lambda t: -hops(*t))

    for d in range(1, lon_parts):
        tell(barrier, lat - core, (lon + d) % lon_parts)

    @pl.when(is_high)
    def _():
        tell(barrier, lat - 1, lon)

    @pl.when(is_high & has_high)
    def _():
        tell(barrier, lat + 1, lon)

    @pl.when(is_low & has_low)
    def _():
        tell(barrier, lat - 2, lon)

    own_block = fields.at[:, pl.ds(lon * chans, chans), :]
    pairs = (
        (raw_h, raw), (values_h, values), (row_off_h, row_off), (col_off_h, col_off),
        (sizes_h, sizes), (shift_table, shift), (own_block, blocks.at[lon]), (fourier, four),
        (per_lat_h, per_lat), (scalars_h, scalars),
    )
    fetches = [pltpu.make_async_copy(p, q, sem_in.at[n]) for n, (p, q) in enumerate(pairs)]
    for fetch in fetches:
        fetch.start()

    @pl.when(is_low)
    def _():
        sides = has_low.astype(jnp.int32) + (lat < lat_parts - 2).astype(jnp.int32)
        pl.semaphore_wait(barrier, 2 * (lon_parts - 1) + 1 + sides)
        tell(near, lat + 1, lon)

    @pl.when(is_high)
    def _():
        pl.semaphore_wait(near, 1)

    lon_copies = []
    for d in (1, lon_parts - 1, 2):
        other = (lon + d) % lon_parts
        copy = pltpu.make_async_remote_copy(
            src_ref=fields.at[:, pl.ds(other * chans, chans), :],
            dst_ref=blocks.at[lon],
            send_sem=sem_lon_s.at[d - 1],
            recv_sem=sem_lon_r.at[d - 1],
            device_id=(lat, other),
            device_id_type=MESH,
        )
        copy.start()
        lon_copies.append((d, copy))

    @pl.when(is_low)
    def _():
        for turn in turns[0::2]:
            tell(barrier, far_chip(*turn) * 2 + 1, lon)

    @pl.when(is_high)
    def _():
        for turn in turns[1::2]:
            tell(barrier, far_chip(*turn) * 2 + 1, lon)

    for fetch in fetches[:6]:
        fetch.wait()
    cells = lax.broadcasted_iota(jnp.int32, (1, 2 * HALF), 1) % HALF
    meta_v[...] = jnp.zeros_like(meta_v)
    meta_r[...] = jnp.zeros_like(meta_r)
    meta_c[...] = jnp.zeros_like(meta_c)
    for at in (0, HALF):
        meta_v[:, at : at + SUPPORT] = values[...]
        meta_r[:, at : at + SUPPORT] = row_off[...]
        meta_c[:, at : at + SUPPORT] = col_off[...]
    wide_w[...] = jnp.zeros_like(wide_w)
    flat = raw[...].astype(f32).reshape(SUPPORT * GROUP, raw.shape[2])
    for at in (0, HALF * GROUP):
        wide_w[at : at + SUPPORT * GROUP, : raw.shape[2]] = flat
    for a in range(GROUP):
        turned[...] = wide_w[pl.ds(a, 2 * HALF, stride=GROUP), :].T
        own_turned[a * chans : (a + 1) * chans, :] = turned[
            pl.ds(pl.multiple_of(lon * chans, chans), chans), :
        ]
    for o in range(chans):
        weights[o * GROUP : (o + 1) * GROUP, :] = own_turned[pl.ds(o, GROUP, stride=chans), :]
    weights_f32 = weights[...]
    shift_row = lax.broadcasted_iota(jnp.int32, (2 * HALF, 2 * HALF), 0)
    shift_lane = lax.broadcasted_iota(jnp.int32, (2 * HALF, 2 * HALF), 1)
    same_half = shift_row // HALF == shift_lane // HALF
    shift_of_row = shift_row % HALF - LON_REACH
    for i in range(lat_dev):
        live = (cells < sizes[i]).astype(f32)
        scaled = meta_v[i : i + 1, :] * live
        effective = (weights_f32 * scaled).astype(bf16).astype(f32)
        rows_of = meta_r[i : i + 1, :]
        for r in range(ROWS):
            left[r * 128 : (r + 1) * 128, :] = jnp.where(
                rows_of == r - LAT_REACH, effective, 0.0
            ).astype(bf16)
        pick = (same_half & (shift_of_row == meta_c[i : i + 1, :])).astype(f32).astype(bf16)
        phases = jnp.dot(shift[...], pick, preferred_element_type=f32).astype(bf16)
        w[i] = lax.dot_general(left[...], phases, NT, preferred_element_type=f32)

    def transform(block):
        data = blocks[block].reshape(lat_dev * chans, blocks.shape[3])
        part = jnp.dot(data, four[block], preferred_element_type=f32)
        return part.reshape(lat_dev, chans, 2 * deg)

    fetches[6].wait()
    fetches[7].wait()
    own = pl.ds(LAT_REACH, lat_dev)
    xs[own] = transform(lon)
    for d, copy in lon_copies:
        copy.wait_recv()
        xs[own] += transform((lon + lon_parts - d) % lon_parts)

    up = pltpu.make_async_remote_copy(
        src_ref=xs.at[pl.ds(lat_dev, LAT_REACH)],
        dst_ref=xs.at[pl.ds(0, LAT_REACH)],
        send_sem=sem_halo_s.at[0],
        recv_sem=sem_halo_r.at[0],
        device_id=((lat + 1) % lat_parts, lon),
        device_id_type=MESH,
    )
    down = pltpu.make_async_remote_copy(
        src_ref=xs.at[pl.ds(LAT_REACH, LAT_REACH)],
        dst_ref=xs.at[pl.ds(LAT_REACH + lat_dev, LAT_REACH)],
        send_sem=sem_halo_s.at[1],
        recv_sem=sem_halo_r.at[1],
        device_id=((lat + lat_parts - 1) % lat_parts, lon),
        device_id_type=MESH,
    )

    @pl.when(has_high)
    def _():
        up.start()

    @pl.when(has_low)
    def _():
        down.start()

    @pl.when(jnp.logical_not(has_low))
    def _():
        xs[0:LAT_REACH] = jnp.zeros((LAT_REACH,) + xs.shape[1:], f32)

    @pl.when(jnp.logical_not(has_high))
    def _():
        xs[LAT_REACH + lat_dev :] = jnp.zeros((LAT_REACH,) + xs.shape[1:], f32)

    groups = chans // GROUP

    def products(i, g, o, rows, x_rows):
        real = imag = None
        at = pl.multiple_of(g * (GROUP * GROUP), GROUP * GROUP) + o * GROUP
        for row, (xr, xi) in zip(rows, x_rows):
            tile = w[i, pl.ds(pl.multiple_of((row - i) * 128 + at, GROUP), GROUP), :]
            wr, wi = tile[:, :deg], tile[:, deg:]
            re, im = wr * xr - wi * xi, wr * xi + wi * xr
            real, imag = (re, im) if real is None else (real + re, imag + im)
        return real, imag

    def load_rows(rows, g):
        tiles = [xs[row, pl.ds(pl.multiple_of(g * GROUP, GROUP), GROUP), :] for row in rows]
        return [(t[:, :deg], t[:, deg:]) for t in tiles]

    def own_rows(ig, carry):
        i, g = ig // groups, ig % groups
        rows = [LAT_REACH + j for j in range(lat_dev)]
        x_rows = load_rows(rows, g)
        for o in range(GROUP):
            real, imag = products(i, g, o, rows, x_rows)
            acc[ig, o * GROUP : (o + 1) * GROUP, :deg] = real
            acc[ig, o * GROUP : (o + 1) * GROUP, deg:] = imag
        return carry

    lax.fori_loop(0, lat_dev * groups, own_rows, 0)

    @pl.when(has_low)
    def _():
        up.wait_recv()

    @pl.when(has_high)
    def _():
        down.wait_recv()

    def other_rows(ig, carry):
        i, g = ig // groups, ig % groups
        rows = [i + j + lat_dev * ((i + j) // LAT_REACH) for j in range(LAT_REACH)]
        x_rows = load_rows(rows, g)
        for o in range(GROUP):
            real, imag = products(i, g, o, rows, x_rows)
            real += acc[ig, o * GROUP : (o + 1) * GROUP, :deg]
            imag += acc[ig, o * GROUP : (o + 1) * GROUP, deg:]
            z[ig, 2 * o : 2 * o + 1, :] = jnp.sum(real, axis=0, keepdims=True)
            z[ig, 2 * o + 1 : 2 * o + 2, :] = jnp.sum(imag, axis=0, keepdims=True)
        return carry

    lax.fori_loop(0, lat_dev * groups, other_rows, 0)

    @pl.when(has_high)
    def _():
        up.wait_send()

    @pl.when(has_low)
    def _():
        down.wait_send()

    by_order = z[...].reshape(128, deg).T.astype(bf16)
    send_a[...] = by_order.reshape(chips, 4, 128)

    @pl.when(is_high)
    def _():
        pl.semaphore_wait(barrier, chips - 1)
        tell(far, lat - 1, lon)

    @pl.when(is_low)
    def _():
        pl.semaphore_wait(far, 1)

    a_copies = []
    for n, turn in enumerate(turns):
        other = far_chip(*turn)
        copy = pltpu.make_async_remote_copy(
            src_ref=send_a.at[other],
            dst_ref=recv_a.at[chip],
            send_sem=sem_a_s.at[n],
            recv_sem=sem_a_r.at[n],
            device_id=(other * 2 + core, lon),
            device_id_type=MESH,
        )
        copy.start()
        a_copies.append(copy)
    recv_a[chip] = send_a[chip]

    fetches[8].wait()
    fetches[9].wait()
    half = lax.broadcasted_iota(jnp.int32, (8, lat_parts), 0) // lat_dev
    orders = (2 * lat + half).astype(f32)
    order_square = orders * orders
    cosine, log_sine, weight = per_lat[0], per_lat[1], per_lat[2]
    norm = jnp.where(half == 0, scalars[2 * deg + 2 * lat], scalars[2 * deg + 2 * lat + 1])
    start = jnp.exp(norm + orders * log_sine)

    def advance(l, state):
        previous, before, inverse, degree = state
        denominator = degree * degree - order_square
        root = lax.rsqrt(jnp.maximum(denominator, 1.0))
        first = jnp.where(denominator > 0.0, scalars[l] * root, 0.0)
        second = first * inverse
        fresh = first * cosine * previous - second * before
        fresh += jnp.where(denominator == 0.0, start, 0.0)
        table[pl.ds(pl.multiple_of(l * 8, 8), 8), :] = fresh * weight
        inverse = jnp.maximum(denominator, 0.0) * root * scalars[deg + l]
        return fresh, previous, inverse, degree + 1.0

    zeros = cosine * 0.0
    lax.fori_loop(0, deg, advance, (zeros, zeros, zeros, zeros), unroll=8)

    for s in range(8):
        exact = table[pl.ds(s, deg, stride=8), :]
        high = exact.astype(bf16)
        tcat[s, :, :lat_parts] = high
        tcat[s, :, lat_parts:] = (exact - high.astype(f32)).astype(bf16)

    for copy in a_copies:
        copy.wait_send()
    for copy in a_copies:
        copy.wait_recv()

    wide_a[...] = recv_a[...].astype(f32).reshape(deg, 128)
    rows = [wide_a[pl.ds(j, chips, stride=4), :] for j in range(4)]
    for m in range(2):
        send_b[m] = jnp.where(is_low, rows[2 + m], rows[m]).astype(bf16)
    swap = pltpu.make_async_remote_copy(
        src_ref=send_b,
        dst_ref=recv_b.at[core],
        send_sem=sem_b_s.at[0],
        recv_sem=sem_b_r.at[0],
        device_id=(lat + 1 - 2 * core, lon),
        device_id_type=MESH,
    )
    swap.start()
    for m in range(2):
        recv_b[core, m] = jnp.where(is_low, rows[m], rows[2 + m]).astype(bf16)
    swap.wait_recv()

    for m in range(2):
        of_order = recv_b[:, m].astype(f32).reshape(lat_parts, 128)
        by_lat = of_order.T.astype(bf16)
        total = None
        for i in range(lat_dev):
            part = by_lat[i * 32 : (i + 1) * 32, :]
            part = jnp.concatenate([part, part], axis=1)
            term = lax.dot_general(part, tcat[m * lat_dev + i], NT, preferred_element_type=f32)
            total = term if total is None else total + term
        out[0, :, :, m, :] = total.reshape(chans, 2, deg)

    for _, copy in lon_copies:
        copy.wait_send()

    swap.wait_send()


def body(consts, fields, filter_weights, filter_values, row_offsets, col_offsets, support_sizes):
    _, lat_dev, all_chans, lon_dev = fields.shape
    lat_parts, lon_parts = lax.axis_size("lat"), lax.axis_size("lon")
    chans, deg, chips = all_chans // lon_parts, 2 * lat_parts, lat_parts // 2
    vmem, hbm = pl.BlockSpec(memory_space=pltpu.VMEM), pl.BlockSpec(memory_space=pltpu.HBM)
    f32, bf16, dma = jnp.float32, jnp.bfloat16, pltpu.SemaphoreType.DMA
    return pl.pallas_call(
        kernel,
        out_shape=jax.ShapeDtypeStruct((1, chans, 2, 2, deg), f32),
        in_specs=[hbm] * 10,
        out_specs=vmem,
        scratch_shapes=[
            pltpu.VMEM((SUPPORT, GROUP, all_chans), bf16),
            pltpu.VMEM((lat_dev, SUPPORT), f32),
            pltpu.VMEM((lat_dev, SUPPORT), jnp.int32),
            pltpu.VMEM((lat_dev, SUPPORT), jnp.int32),
            pltpu.SMEM((lat_dev,), jnp.int32),
            pltpu.VMEM((3, 8, lat_parts), f32),
            pltpu.SMEM((3 * deg,), f32),
            pltpu.VMEM((2 * HALF * GROUP, 128), f32),
            pltpu.VMEM((128, 2 * HALF), f32),
            pltpu.VMEM((chans * GROUP, 2 * HALF), f32),
            pltpu.VMEM((chans * GROUP, 2 * HALF), f32),
            pltpu.VMEM((lon_parts, lat_dev, chans, lon_dev), bf16),
            pltpu.VMEM((lon_parts, lon_dev, 2 * deg), bf16),
            pltpu.VMEM((2 * deg, 2 * HALF), bf16),
            pltpu.VMEM((lat_dev + 2 * LAT_REACH, chans, 2 * deg), f32),
            pltpu.VMEM((lat_dev, 2 * HALF), f32),
            pltpu.VMEM((lat_dev, 2 * HALF), jnp.int32),
            pltpu.VMEM((lat_dev, 2 * HALF), jnp.int32),
            pltpu.VMEM((ROWS * chans * GROUP, 2 * HALF), bf16),
            pltpu.VMEM((lat_dev, ROWS * chans * GROUP, 2 * deg), f32),
            pltpu.VMEM((lat_dev * chans // GROUP, GROUP * GROUP, 2 * deg), f32),
            pltpu.VMEM((lat_dev * chans // GROUP, 2 * GROUP, deg), f32),
            pltpu.VMEM((chips, 4, 128), bf16),
            pltpu.VMEM((chips, 4, 128), bf16),
            pltpu.VMEM((deg, 128), f32),
            pltpu.VMEM((2, chips, 128), bf16),
            pltpu.VMEM((2, 2, chips, 128), bf16),
            pltpu.VMEM((deg * 8, lat_parts), f32),
            pltpu.VMEM((8, deg, 2 * lat_parts), bf16),
            pltpu.SemaphoreType.REGULAR,
            pltpu.SemaphoreType.REGULAR,
            dma((10,)),
            dma((lon_parts - 1,)),
            dma((lon_parts - 1,)),
            dma((2,)),
            dma((2,)),
            dma((chips - 1,)),
            dma((chips - 1,)),
            dma((1,)),
            dma((1,)),
        ],
        compiler_params=pltpu.CompilerParams(
            collective_id=0, has_side_effects=True, vmem_limit_bytes=60 * 1024 * 1024
        ),
    )(
        fields[0], filter_weights.transpose(0, 2, 1), filter_values, row_offsets, col_offsets, support_sizes,
        *(jnp.asarray(c) for c in consts),
    )


def solution(mesh):
    placed = (
        P(None, "lat", None, "lon"),
        P(),
        P("lat", None),
        P("lat", None),
        P("lat", None),
        P("lat"),
    )

    def whole(fields, *rest):
        lat_parts, lon_parts = mesh.shape["lat"], mesh.shape["lon"]
        consts = tables(
            lat_parts, lon_parts, fields.shape[3] // lon_parts, fields.shape[1] // lat_parts
        )
        return jax.shard_map(
            functools.partial(body, consts),
            mesh=mesh,
            in_specs=placed,
            out_specs=P(None, "lon", None, "lat", None),
            check_vma=False,
        )(fields, *rest)

    return whole
```

```python
import functools
import math

import jax
import jax.numpy as jnp
import ml_dtypes
import numpy as np
from jax import lax
from jax.experimental import pallas as pl
from jax.experimental.pallas import tpu as pltpu
from jax.sharding import PartitionSpec as P

GROUP = 8
SUPPORT = 49
LAT_REACH = 3
LON_REACH = 16
ROWS = 2 * LAT_REACH + 1
HALF = 64
Z = 8
MESH = pl.DeviceIdType.MESH
NT = (((1,), (1,)), ((), ()))


def far_first(count):
    return sorted(range(1, count), key=lambda d: -min(d, count - d))


def split(x):
    high = x.astype(ml_dtypes.bfloat16)
    low = (x - high.astype(np.float64)).astype(ml_dtypes.bfloat16)
    return high, low


def tables(lat_parts, lon_parts, lon_dev, lat_dev):
    nlon, nlat, deg = lon_parts * lon_dev, lat_parts * lat_dev, 2 * lat_parts
    orders = np.arange(deg)
    phase = 2.0 * math.pi / nlon * ((np.arange(nlon)[:, None] * orders[None, :]) % nlon)
    fourier = np.concatenate([np.cos(phase), -np.sin(phase)], 1).astype(ml_dtypes.bfloat16)
    fourier = fourier.reshape(lon_parts, lon_dev, 2 * deg)
    shifts = np.arange(-LON_REACH, LON_REACH + 1)
    turn = 2.0 * math.pi / nlon * ((orders[:, None] * shifts[None, :]) % nlon)
    turn = np.concatenate([np.cos(turn), np.sin(turn)], 0)
    shift_table = np.zeros((2 * deg, 2 * HALF), ml_dtypes.bfloat16)
    shift_table[:, : shifts.size], shift_table[:, HALF : HALF + shifts.size] = split(turn)
    y_count, lane = lat_parts // (2 * Z), np.arange(lat_parts)
    band = (lane % y_count) * 2 * Z + lane // y_count
    lats = lat_dev * band[None, :] + (np.arange(8) % lat_dev)[:, None]
    colat = math.pi * (lats + 0.5) / nlat
    per_lat = np.stack([np.cos(colat), np.log(np.sin(colat)), math.pi / nlat * np.sin(colat)])
    factors = np.arange(1, deg)
    log_product = np.concatenate([[0.0], np.cumsum(np.log((2.0 * factors - 1) / (2.0 * factors)))])
    log_norm = 0.5 * (np.log((2.0 * orders + 1) / (4 * math.pi)) + log_product)
    grow = np.sqrt(np.maximum(4.0 * orders * orders - 1, 1.0))
    scalars = np.concatenate([grow, 1.0 / grow, log_norm])
    return fourier, shift_table, per_lat.astype(np.float32), scalars.astype(np.float32)


def kernel(
    fields, raw_h, values_h, row_off_h, col_off_h, sizes_h, fourier, shift_table, per_lat_h, scalars_h,
    out,
    raw, values, row_off, col_off, sizes, per_lat, scalars, wide_w, turned, own_turned, weights,
    blocks, four, shift, xs, meta_v, meta_r, meta_c, left, w, acc, z, send_a, recv_a, wide_a, send_b, recv_b,
    table, tcat,
    near, far, sem_in, sem_lon_s, sem_lon_r, sem_halo_s, sem_halo_r, sem_a_s, sem_a_r, sem_b_s, sem_b_r,
):
    lat, lon = lax.axis_index("lat"), lax.axis_index("lon")
    lat_parts, lon_parts = lax.axis_size("lat"), lax.axis_size("lon")
    y_count, zc_count = lat_parts // (2 * Z), 2 * Z
    chip, core, y, zc = lat // 2, lat % 2, lat // zc_count, lat % zc_count
    lat_dev, chans = blocks.shape[1], blocks.shape[2]
    deg = 2 * lat_parts
    f32, bf16 = jnp.float32, jnp.bfloat16

    barrier = pltpu.get_barrier_semaphore()
    is_low, is_high = core == 0, core == 1
    has_low, has_high = lat > 0, lat < lat_parts - 1

    def tell(sem, to_lat, to_lon):
        pl.semaphore_signal(sem, 1, device_id=(to_lat, to_lon), device_id_type=MESH)

    def ahead(at, step, count):
        return jnp.where(at + step >= count, at + step - count, at + step)

    for d in range(1, lon_parts):
        tell(barrier, lat - core, ahead(lon, d, lon_parts))

    @pl.when(is_high)
    def _():
        tell(barrier, lat - 1, lon)

    @pl.when(is_high & has_high)
    def _():
        tell(barrier, lat + 1, lon)

    @pl.when(is_low & has_low)
    def _():
        tell(barrier, lat - 2, lon)

    @pl.when(is_low)
    def _():
        sides = has_low.astype(jnp.int32) + (lat < lat_parts - 2).astype(jnp.int32)
        pl.semaphore_wait(barrier, 2 * (lon_parts - 1) + 1 + sides)
        tell(near, lat + 1, lon)

    @pl.when(is_high)
    def _():
        pl.semaphore_wait(near, 1)

    lon_copies = []
    for d in (1, lon_parts - 1, 2):
        other = ahead(lon, d, lon_parts)
        copy = pltpu.make_async_remote_copy(
            src_ref=fields.at[:, pl.ds(other * chans, chans), :],
            dst_ref=blocks.at[lon],
            send_sem=sem_lon_s.at[d - 1],
            recv_sem=sem_lon_r.at[d - 1],
            device_id=(lat, other),
            device_id_type=MESH,
        )
        copy.start()
        lon_copies.append((d, copy))

    own_block = fields.at[:, pl.ds(lon * chans, chans), :]
    pairs = (
        (raw_h, raw), (values_h, values), (row_off_h, row_off), (col_off_h, col_off),
        (sizes_h, sizes), (shift_table, shift), (own_block, blocks.at[lon]), (fourier, four),
        (per_lat_h, per_lat), (scalars_h, scalars),
    )
    fetches = [pltpu.make_async_copy(p, q, sem_in.at[n]) for n, (p, q) in enumerate(pairs)]
    for fetch in fetches:
        fetch.start()

    @pl.when(is_low)
    def _():
        for d in far_first(y_count):
            tell(barrier, ahead(y, d, y_count) * zc_count + zc + 1, lon)

    @pl.when(is_high)
    def _():
        for d in far_first(Z):
            tell(barrier, y * zc_count + ahead(zc, 2 * d, zc_count), lon)

    for fetch in fetches[:6]:
        fetch.wait()
    cells = lax.broadcasted_iota(jnp.int32, (1, 2 * HALF), 1) % HALF
    meta_v[...] = jnp.zeros_like(meta_v)
    meta_r[...] = jnp.zeros_like(meta_r)
    meta_c[...] = jnp.zeros_like(meta_c)
    for at in (0, HALF):
        meta_v[:, at : at + SUPPORT] = values[...]
        meta_r[:, at : at + SUPPORT] = row_off[...]
        meta_c[:, at : at + SUPPORT] = col_off[...]
    wide_w[...] = jnp.zeros_like(wide_w)
    flat = raw[...].astype(f32).reshape(SUPPORT * GROUP, raw.shape[2])
    for at in (0, HALF * GROUP):
        wide_w[at : at + SUPPORT * GROUP, : raw.shape[2]] = flat
    for a in range(GROUP):
        turned[...] = wide_w[pl.ds(a, 2 * HALF, stride=GROUP), :].T
        own_turned[a * chans : (a + 1) * chans, :] = turned[
            pl.ds(pl.multiple_of(lon * chans, chans), chans), :
        ]
    for o in range(chans):
        weights[o * GROUP : (o + 1) * GROUP, :] = own_turned[pl.ds(o, GROUP, stride=chans), :]
    weights_f32 = weights[...]
    shift_row = lax.broadcasted_iota(jnp.int32, (2 * HALF, 2 * HALF), 0)
    shift_lane = lax.broadcasted_iota(jnp.int32, (2 * HALF, 2 * HALF), 1)
    same_half = shift_row // HALF == shift_lane // HALF
    shift_of_row = shift_row % HALF - LON_REACH
    for i in range(lat_dev):
        live = (cells < sizes[i]).astype(f32)
        scaled = meta_v[i : i + 1, :] * live
        effective = (weights_f32 * scaled).astype(bf16).astype(f32)
        rows_of = meta_r[i : i + 1, :]
        for r in range(ROWS):
            left[r * 128 : (r + 1) * 128, :] = jnp.where(
                rows_of == r - LAT_REACH, effective, 0.0
            ).astype(bf16)
        pick = (same_half & (shift_of_row == meta_c[i : i + 1, :])).astype(f32).astype(bf16)
        phases = jnp.dot(shift[...], pick, preferred_element_type=f32).astype(bf16)
        w[i] = lax.dot_general(left[...], phases, NT, preferred_element_type=f32)

    def transform(block):
        data = blocks[block].reshape(lat_dev * chans, blocks.shape[3])
        part = jnp.dot(data, four[block], preferred_element_type=f32)
        return part.reshape(lat_dev, chans, 2 * deg)

    fetches[6].wait()
    fetches[7].wait()
    own = pl.ds(LAT_REACH, lat_dev)
    xs[own] = transform(lon)
    for d, copy in lon_copies:
        copy.wait_recv()
        xs[own] += transform((lon + lon_parts - d) % lon_parts)

    up = pltpu.make_async_remote_copy(
        src_ref=xs.at[pl.ds(lat_dev, LAT_REACH)],
        dst_ref=xs.at[pl.ds(0, LAT_REACH)],
        send_sem=sem_halo_s.at[0],
        recv_sem=sem_halo_r.at[0],
        device_id=((lat + 1) % lat_parts, lon),
        device_id_type=MESH,
    )
    down = pltpu.make_async_remote_copy(
        src_ref=xs.at[pl.ds(LAT_REACH, LAT_REACH)],
        dst_ref=xs.at[pl.ds(LAT_REACH + lat_dev, LAT_REACH)],
        send_sem=sem_halo_s.at[1],
        recv_sem=sem_halo_r.at[1],
        device_id=((lat + lat_parts - 1) % lat_parts, lon),
        device_id_type=MESH,
    )

    @pl.when(has_high)
    def _():
        up.start()

    @pl.when(has_low)
    def _():
        down.start()

    @pl.when(jnp.logical_not(has_low))
    def _():
        xs[0:LAT_REACH] = jnp.zeros((LAT_REACH,) + xs.shape[1:], f32)

    @pl.when(jnp.logical_not(has_high))
    def _():
        xs[LAT_REACH + lat_dev :] = jnp.zeros((LAT_REACH,) + xs.shape[1:], f32)

    groups = chans // GROUP

    def products(i, g, o, rows, x_rows):
        real = imag = None
        at = pl.multiple_of(g * (GROUP * GROUP), GROUP * GROUP) + o * GROUP
        for row, (xr, xi) in zip(rows, x_rows):
            tile = w[i, pl.ds(pl.multiple_of((row - i) * 128 + at, GROUP), GROUP), :]
            wr, wi = tile[:, :deg], tile[:, deg:]
            re, im = wr * xr - wi * xi, wr * xi + wi * xr
            real, imag = (re, im) if real is None else (real + re, imag + im)
        return real, imag

    def load_rows(rows, g):
        tiles = [xs[row, pl.ds(pl.multiple_of(g * GROUP, GROUP), GROUP), :] for row in rows]
        return [(t[:, :deg], t[:, deg:]) for t in tiles]

    def own_rows(ig, carry):
        i, g = ig // groups, ig % groups
        rows = [LAT_REACH + j for j in range(lat_dev)]
        x_rows = load_rows(rows, g)
        for o in range(GROUP):
            real, imag = products(i, g, o, rows, x_rows)
            acc[ig, o * GROUP : (o + 1) * GROUP, :deg] = real
            acc[ig, o * GROUP : (o + 1) * GROUP, deg:] = imag
        return carry

    lax.fori_loop(0, lat_dev * groups, own_rows, 0)

    @pl.when(has_low)
    def _():
        up.wait_recv()

    @pl.when(has_high)
    def _():
        down.wait_recv()

    def other_rows(ig, carry):
        i, g = ig // groups, ig % groups
        rows = [i + j + lat_dev * ((i + j) // LAT_REACH) for j in range(LAT_REACH)]
        x_rows = load_rows(rows, g)
        for o in range(GROUP):
            real, imag = products(i, g, o, rows, x_rows)
            real += acc[ig, o * GROUP : (o + 1) * GROUP, :deg]
            imag += acc[ig, o * GROUP : (o + 1) * GROUP, deg:]
            z[ig, 2 * o : 2 * o + 1, :] = jnp.sum(real, axis=0, keepdims=True)
            z[ig, 2 * o + 1 : 2 * o + 2, :] = jnp.sum(imag, axis=0, keepdims=True)
        return carry

    lax.fori_loop(0, lat_dev * groups, other_rows, 0)

    @pl.when(has_high)
    def _():
        up.wait_send()

    @pl.when(has_low)
    def _():
        down.wait_send()

    by_order = z[...].reshape(128, deg).T.astype(bf16)
    send_a[...] = by_order.reshape(y_count, zc_count * 2, 128)

    @pl.when(is_high)
    def _():
        pl.semaphore_wait(barrier, y_count - 1 + Z - 1)
        tell(far, lat - 1, lon)

    @pl.when(is_low)
    def _():
        pl.semaphore_wait(far, 1)

    a_copies = []
    for d in far_first(y_count):
        other = ahead(y, d, y_count)
        copy = pltpu.make_async_remote_copy(
            src_ref=send_a.at[other],
            dst_ref=recv_a.at[y],
            send_sem=sem_a_s.at[d - 1],
            recv_sem=sem_a_r.at[d - 1],
            device_id=(other * zc_count + zc, lon),
            device_id_type=MESH,
        )
        copy.start()
        a_copies.append(copy)
    recv_a[y] = send_a[y]

    fetches[8].wait()
    fetches[9].wait()
    half = lax.broadcasted_iota(jnp.int32, (8, lat_parts), 0) // lat_dev
    orders = (2 * lat + half).astype(f32)
    order_square = orders * orders
    cosine, log_sine, weight = per_lat[0], per_lat[1], per_lat[2]
    norm = jnp.where(half == 0, scalars[2 * deg + 2 * lat], scalars[2 * deg + 2 * lat + 1])
    start = jnp.exp(norm + orders * log_sine)

    def advance(l, state):
        previous, before, inverse, degree = state
        denominator = degree * degree - order_square
        root = lax.rsqrt(jnp.maximum(denominator, 1.0))
        first = jnp.where(denominator > 0.0, scalars[l] * root, 0.0)
        second = first * inverse
        fresh = first * cosine * previous - second * before
        fresh += jnp.where(denominator == 0.0, start, 0.0)
        table[pl.ds(pl.multiple_of(l * 8, 8), 8), :] = fresh * weight
        inverse = jnp.maximum(denominator, 0.0) * root * scalars[deg + l]
        return fresh, previous, inverse, degree + 1.0

    zeros = cosine * 0.0
    lax.fori_loop(0, deg, advance, (zeros, zeros, zeros, zeros), unroll=8)

    for s in range(8):
        exact = table[pl.ds(s, deg, stride=8), :]
        high = exact.astype(bf16)
        tcat[s, :, :lat_parts] = high
        tcat[s, :, lat_parts:] = (exact - high.astype(f32)).astype(bf16)

    for copy in a_copies:
        copy.wait_send()
    for copy in a_copies:
        copy.wait_recv()

    wide_a[...] = recv_a[...].astype(f32).reshape(deg, 128)
    b_copies = []
    for d in [2 * d + e for d in far_first(Z) for e in (0, 1)] + [1, 0]:
        other = ahead(zc, d, zc_count)
        low = wide_a[pl.ds(2 * other, y_count, stride=2 * zc_count), :]
        high = wide_a[pl.ds(2 * other + 1, y_count, stride=2 * zc_count), :]
        tile = jnp.concatenate([low, high], axis=0).astype(bf16)
        if d == 0:
            recv_b[zc] = tile
            continue
        send_b[other] = tile
        copy = pltpu.make_async_remote_copy(
            src_ref=send_b.at[other],
            dst_ref=recv_b.at[zc],
            send_sem=sem_b_s.at[d - 1],
            recv_sem=sem_b_r.at[d - 1],
            device_id=(y * zc_count + other, lon),
            device_id_type=MESH,
        )
        copy.start()
        b_copies.append(copy)

    for _, copy in lon_copies:
        copy.wait_send()
    for copy in b_copies:
        copy.wait_recv()

    arrived = recv_b[...].astype(f32)
    for m in range(2):
        of_order = arrived[:, m * y_count : (m + 1) * y_count, :].reshape(lat_parts, 128)
        by_lat = of_order.T.astype(bf16)
        total = None
        for i in range(lat_dev):
            part = by_lat[i * 32 : (i + 1) * 32, :]
            part = jnp.concatenate([part, part], axis=1)
            term = lax.dot_general(part, tcat[m * lat_dev + i], NT, preferred_element_type=f32)
            total = term if total is None else total + term
        out[0, :, :, m, :] = total.reshape(chans, 2, deg)

    for copy in b_copies:
        copy.wait_send()


def body(consts, fields, filter_weights, filter_values, row_offsets, col_offsets, support_sizes):
    _, lat_dev, all_chans, lon_dev = fields.shape
    lat_parts, lon_parts = lax.axis_size("lat"), lax.axis_size("lon")
    chans, deg = all_chans // lon_parts, 2 * lat_parts
    y_count, zc_count = lat_parts // (2 * Z), 2 * Z
    vmem, hbm = pl.BlockSpec(memory_space=pltpu.VMEM), pl.BlockSpec(memory_space=pltpu.HBM)
    f32, bf16, dma = jnp.float32, jnp.bfloat16, pltpu.SemaphoreType.DMA
    return pl.pallas_call(
        kernel,
        out_shape=jax.ShapeDtypeStruct((1, chans, 2, 2, deg), f32),
        in_specs=[hbm] * 10,
        out_specs=vmem,
        scratch_shapes=[
            pltpu.VMEM((SUPPORT, GROUP, all_chans), bf16),
            pltpu.VMEM((lat_dev, SUPPORT), f32),
            pltpu.VMEM((lat_dev, SUPPORT), jnp.int32),
            pltpu.VMEM((lat_dev, SUPPORT), jnp.int32),
            pltpu.SMEM((lat_dev,), jnp.int32),
            pltpu.VMEM((3, 8, lat_parts), f32),
            pltpu.SMEM((3 * deg,), f32),
            pltpu.VMEM((2 * HALF * GROUP, 128), f32),
            pltpu.VMEM((128, 2 * HALF), f32),
            pltpu.VMEM((chans * GROUP, 2 * HALF), f32),
            pltpu.VMEM((chans * GROUP, 2 * HALF), f32),
            pltpu.VMEM((lon_parts, lat_dev, chans, lon_dev), bf16),
            pltpu.VMEM((lon_parts, lon_dev, 2 * deg), bf16),
            pltpu.VMEM((2 * deg, 2 * HALF), bf16),
            pltpu.VMEM((lat_dev + 2 * LAT_REACH, chans, 2 * deg), f32),
            pltpu.VMEM((lat_dev, 2 * HALF), f32),
            pltpu.VMEM((lat_dev, 2 * HALF), jnp.int32),
            pltpu.VMEM((lat_dev, 2 * HALF), jnp.int32),
            pltpu.VMEM((ROWS * chans * GROUP, 2 * HALF), bf16),
            pltpu.VMEM((lat_dev, ROWS * chans * GROUP, 2 * deg), f32),
            pltpu.VMEM((lat_dev * chans // GROUP, GROUP * GROUP, 2 * deg), f32),
            pltpu.VMEM((lat_dev * chans // GROUP, 2 * GROUP, deg), f32),
            pltpu.VMEM((y_count, 2 * zc_count, 128), bf16),
            pltpu.VMEM((y_count, 2 * zc_count, 128), bf16),
            pltpu.VMEM((deg, 128), f32),
            pltpu.VMEM((zc_count, 2 * y_count, 128), bf16),
            pltpu.VMEM((zc_count, 2 * y_count, 128), bf16),
            pltpu.VMEM((deg * 8, lat_parts), f32),
            pltpu.VMEM((8, deg, 2 * lat_parts), bf16),
            pltpu.SemaphoreType.REGULAR,
            pltpu.SemaphoreType.REGULAR,
            dma((10,)),
            dma((lon_parts - 1,)),
            dma((lon_parts - 1,)),
            dma((2,)),
            dma((2,)),
            dma((y_count - 1,)),
            dma((y_count - 1,)),
            dma((zc_count - 1,)),
            dma((zc_count - 1,)),
        ],
        compiler_params=pltpu.CompilerParams(
            collective_id=0, has_side_effects=True, vmem_limit_bytes=60 * 1024 * 1024
        ),
    )(
        fields[0], filter_weights.transpose(0, 2, 1), filter_values, row_offsets, col_offsets, support_sizes,
        *(jnp.asarray(c) for c in consts),
    )


def solution(mesh):
    placed = (
        P(None, "lat", None, "lon"),
        P(),
        P("lat", None),
        P("lat", None),
        P("lat", None),
        P("lat"),
    )

    def whole(fields, *rest):
        lat_parts, lon_parts = mesh.shape["lat"], mesh.shape["lon"]
        consts = tables(
            lat_parts, lon_parts, fields.shape[3] // lon_parts, fields.shape[1] // lat_parts
        )
        return jax.shard_map(
            functools.partial(body, consts),
            mesh=mesh,
            in_specs=placed,
            out_specs=P(None, "lon", None, "lat", None),
            check_vma=False,
        )(fields, *rest)

    return whole
```

```python
import functools
import math

import jax
import jax.numpy as jnp
import ml_dtypes
import numpy as np
from jax import lax
from jax.experimental import pallas as pl
from jax.experimental.pallas import tpu as pltpu
from jax.sharding import PartitionSpec as P

GROUP = 8
SUPPORT = 49
LAT_REACH = 3
LON_REACH = 16
ROWS = 2 * LAT_REACH + 1
HALF = 64
Z = 8
MESH = pl.DeviceIdType.MESH
NT = (((1,), (1,)), ((), ()))


def far_first(count):
    return sorted(range(1, count), key=lambda d: -min(d, count - d))


def corner_first(count):
    return sorted(range(count), key=lambda t: min(t, count - t))


def split(x):
    high = x.astype(ml_dtypes.bfloat16)
    low = (x - high.astype(np.float64)).astype(ml_dtypes.bfloat16)
    return high, low


def tables(lat_parts, lon_parts, lon_dev, lat_dev):
    nlon, nlat, deg = lon_parts * lon_dev, lat_parts * lat_dev, 2 * lat_parts
    orders = np.arange(deg)
    phase = 2.0 * math.pi / nlon * ((np.arange(nlon)[:, None] * orders[None, :]) % nlon)
    fourier = np.concatenate([np.cos(phase), -np.sin(phase)], 1).astype(ml_dtypes.bfloat16)
    fourier = fourier.reshape(lon_parts, lon_dev, 2 * deg)
    shifts = np.arange(-LON_REACH, LON_REACH + 1)
    turn = 2.0 * math.pi / nlon * ((orders[:, None] * shifts[None, :]) % nlon)
    turn = np.concatenate([np.cos(turn), np.sin(turn)], 0)
    shift_table = np.zeros((2 * deg, 2 * HALF), ml_dtypes.bfloat16)
    shift_table[:, : shifts.size], shift_table[:, HALF : HALF + shifts.size] = split(turn)
    y_count, lane = lat_parts // (2 * Z), np.arange(lat_parts)
    band = (lane % y_count) * 2 * Z + lane // y_count
    lats = lat_dev * band[None, :] + (np.arange(8) % lat_dev)[:, None]
    colat = math.pi * (lats + 0.5) / nlat
    per_lat = np.stack([np.cos(colat), np.log(np.sin(colat)), math.pi / nlat * np.sin(colat)])
    factors = np.arange(1, deg)
    log_product = np.concatenate([[0.0], np.cumsum(np.log((2.0 * factors - 1) / (2.0 * factors)))])
    log_norm = 0.5 * (np.log((2.0 * orders + 1) / (4 * math.pi)) + log_product)
    grow = np.sqrt(np.maximum(4.0 * orders * orders - 1, 1.0))
    scalars = np.concatenate([grow, 1.0 / grow, log_norm])
    return fourier, shift_table, per_lat.astype(np.float32), scalars.astype(np.float32)


def kernel(
    fields, raw_h, values_h, row_off_h, col_off_h, sizes_h, fourier, shift_table, per_lat_h, scalars_h,
    out,
    raw, values, row_off, col_off, sizes, per_lat, scalars, wide_w, turned, own_turned, weights,
    blocks, four, shift, edge, beside, xs, meta_v, meta_r, meta_c, left, w, acc, z, send_a, recv_a, wide_a, send_b, recv_b,
    table, tcat,
    near, far, sem_in, sem_lon_s, sem_lon_r, sem_halo_s, sem_halo_r, sem_a_s, sem_a_r, sem_b_s, sem_b_r,
):
    lat, lon = lax.axis_index("lat"), lax.axis_index("lon")
    lat_parts, lon_parts = lax.axis_size("lat"), lax.axis_size("lon")
    y_count, zc_count = lat_parts // (2 * Z), 2 * Z
    chip, core, y, zc = lat // 2, lat % 2, lat // zc_count, lat % zc_count
    lat_dev, chans = blocks.shape[1], blocks.shape[2]
    deg = 2 * lat_parts
    f32, bf16 = jnp.float32, jnp.bfloat16

    barrier = pltpu.get_barrier_semaphore()
    is_low, is_high = core == 0, core == 1
    has_low, has_high = lat > 0, lat < lat_parts - 1

    def tell(sem, to_lat, to_lon):
        pl.semaphore_signal(sem, 1, device_id=(to_lat, to_lon), device_id_type=MESH)

    def ahead(at, step, count):
        return jnp.where(at + step >= count, at + step - count, at + step)

    for d in range(1, lon_parts):
        tell(barrier, lat - core, ahead(lon, d, lon_parts))

    @pl.when(is_high)
    def _():
        tell(barrier, lat - 1, lon)

    @pl.when(is_high & has_high)
    def _():
        tell(barrier, lat + 1, lon)

    @pl.when(is_low & has_low)
    def _():
        tell(barrier, lat - 2, lon)

    @pl.when(is_low)
    def _():
        sides = has_low.astype(jnp.int32) + (lat < lat_parts - 2).astype(jnp.int32)
        pl.semaphore_wait(barrier, 2 * (lon_parts - 1) + 1 + sides)
        tell(near, lat + 1, lon)

    @pl.when(is_high)
    def _():
        pl.semaphore_wait(near, 1)

    lon_copies = []
    for d in (1, lon_parts - 1, 2):
        other = ahead(lon, d, lon_parts)
        copy = pltpu.make_async_remote_copy(
            src_ref=fields.at[:, pl.ds(other * chans, chans), :],
            dst_ref=blocks.at[lon],
            send_sem=sem_lon_s.at[d - 1],
            recv_sem=sem_lon_r.at[d - 1],
            device_id=(lat, other),
            device_id_type=MESH,
        )
        copy.start()
        lon_copies.append((d, copy))

    own_block = fields.at[:, pl.ds(lon * chans, chans), :]
    pairs = (
        (raw_h, raw), (values_h, values), (row_off_h, row_off), (col_off_h, col_off),
        (sizes_h, sizes), (shift_table, shift), (own_block, blocks.at[lon]), (fourier, four),
        (per_lat_h, per_lat), (scalars_h, scalars),
    )
    fetches = [pltpu.make_async_copy(p, q, sem_in.at[n]) for n, (p, q) in enumerate(pairs)]
    for fetch in fetches:
        fetch.start()

    @pl.when(is_low)
    def _():
        for d in far_first(y_count):
            tell(barrier, ahead(y, d, y_count) * zc_count + zc + 1, lon)

    @pl.when(is_high)
    def _():
        for d in far_first(Z):
            tell(barrier, y * zc_count + ahead(zc, 2 * d, zc_count), lon)

    for fetch in fetches[:6]:
        fetch.wait()
    cells = lax.broadcasted_iota(jnp.int32, (1, 2 * HALF), 1) % HALF
    meta_v[...] = jnp.zeros_like(meta_v)
    meta_r[...] = jnp.zeros_like(meta_r)
    meta_c[...] = jnp.zeros_like(meta_c)
    for at in (0, HALF):
        meta_v[:, at : at + SUPPORT] = values[...]
        meta_r[:, at : at + SUPPORT] = row_off[...]
        meta_c[:, at : at + SUPPORT] = col_off[...]
    wide_w[...] = jnp.zeros_like(wide_w)
    flat = raw[...].astype(f32).reshape(SUPPORT * GROUP, raw.shape[2])
    for at in (0, HALF * GROUP):
        wide_w[at : at + SUPPORT * GROUP, : raw.shape[2]] = flat
    for a in range(GROUP):
        turned[...] = wide_w[pl.ds(a, 2 * HALF, stride=GROUP), :].T
        own_turned[a * chans : (a + 1) * chans, :] = turned[
            pl.ds(pl.multiple_of(lon * chans, chans), chans), :
        ]
    for o in range(chans):
        weights[o * GROUP : (o + 1) * GROUP, :] = own_turned[pl.ds(o, GROUP, stride=chans), :]
    weights_f32 = weights[...]
    shift_row = lax.broadcasted_iota(jnp.int32, (2 * HALF, 2 * HALF), 0)
    shift_lane = lax.broadcasted_iota(jnp.int32, (2 * HALF, 2 * HALF), 1)
    same_half = shift_row // HALF == shift_lane // HALF
    shift_of_row = shift_row % HALF - LON_REACH
    for i in range(lat_dev):
        live = (cells < sizes[i]).astype(f32)
        scaled = meta_v[i : i + 1, :] * live
        effective = (weights_f32 * scaled).astype(bf16).astype(f32)
        rows_of = meta_r[i : i + 1, :]
        for r in range(ROWS):
            left[r * 128 : (r + 1) * 128, :] = jnp.where(
                rows_of == r - LAT_REACH, effective, 0.0
            ).astype(bf16)
        pick = (same_half & (shift_of_row == meta_c[i : i + 1, :])).astype(f32).astype(bf16)
        phases = jnp.dot(shift[...], pick, preferred_element_type=f32).astype(bf16)
        w[i] = lax.dot_general(left[...], phases, NT, preferred_element_type=f32)

    def transform(block):
        data = blocks[block].reshape(lat_dev * chans, blocks.shape[3])
        part = jnp.dot(data, four[block], preferred_element_type=f32)
        return part.reshape(lat_dev, chans, 2 * deg)

    fetches[6].wait()
    fetches[7].wait()
    own = pl.ds(LAT_REACH, lat_dev)
    xs[own] = transform(lon)
    for d, copy in lon_copies:
        copy.wait_recv()
        xs[own] += transform((lon + lon_parts - d) % lon_parts)

    edge[...] = xs[own].astype(bf16)
    up = pltpu.make_async_remote_copy(
        src_ref=edge.at[pl.ds(lat_dev - LAT_REACH, LAT_REACH)],
        dst_ref=beside.at[0],
        send_sem=sem_halo_s.at[0],
        recv_sem=sem_halo_r.at[0],
        device_id=((lat + 1) % lat_parts, lon),
        device_id_type=MESH,
    )
    down = pltpu.make_async_remote_copy(
        src_ref=edge.at[pl.ds(0, LAT_REACH)],
        dst_ref=beside.at[1],
        send_sem=sem_halo_s.at[1],
        recv_sem=sem_halo_r.at[1],
        device_id=((lat + lat_parts - 1) % lat_parts, lon),
        device_id_type=MESH,
    )

    @pl.when(has_high)
    def _():
        up.start()

    @pl.when(has_low)
    def _():
        down.start()

    groups = chans // GROUP

    def products(i, g, o, rows, x_rows):
        real = imag = None
        at = pl.multiple_of(g * (GROUP * GROUP), GROUP * GROUP) + o * GROUP
        for row, (xr, xi) in zip(rows, x_rows):
            tile = w[i, pl.ds(pl.multiple_of((row - i) * 128 + at, GROUP), GROUP), :]
            wr, wi = tile[:, :deg], tile[:, deg:]
            re, im = wr * xr - wi * xi, wr * xi + wi * xr
            real, imag = (re, im) if real is None else (real + re, imag + im)
        return real, imag

    def load_rows(rows, g):
        tiles = [xs[row, pl.ds(pl.multiple_of(g * GROUP, GROUP), GROUP), :] for row in rows]
        return [(t[:, :deg], t[:, deg:]) for t in tiles]

    def own_rows(ig, carry):
        i, g = ig // groups, ig % groups
        rows = [LAT_REACH + j for j in range(lat_dev)]
        x_rows = load_rows(rows, g)
        for o in range(GROUP):
            real, imag = products(i, g, o, rows, x_rows)
            acc[ig, o * GROUP : (o + 1) * GROUP, :deg] = real
            acc[ig, o * GROUP : (o + 1) * GROUP, deg:] = imag
        return carry

    lax.fori_loop(0, lat_dev * groups, own_rows, 0)

    @pl.when(has_low)
    def _():
        up.wait_recv()
        xs[:LAT_REACH] = beside[0].astype(f32)

    @pl.when(has_high)
    def _():
        down.wait_recv()
        xs[LAT_REACH + lat_dev :] = beside[1].astype(f32)

    @pl.when(jnp.logical_not(has_low))
    def _():
        xs[:LAT_REACH] = jnp.zeros((LAT_REACH,) + xs.shape[1:], f32)

    @pl.when(jnp.logical_not(has_high))
    def _():
        xs[LAT_REACH + lat_dev :] = jnp.zeros((LAT_REACH,) + xs.shape[1:], f32)

    def other_rows(ig, carry):
        i, g = ig // groups, ig % groups
        rows = [i + j + lat_dev * ((i + j) // LAT_REACH) for j in range(LAT_REACH)]
        x_rows = load_rows(rows, g)
        for o in range(GROUP):
            real, imag = products(i, g, o, rows, x_rows)
            real += acc[ig, o * GROUP : (o + 1) * GROUP, :deg]
            imag += acc[ig, o * GROUP : (o + 1) * GROUP, deg:]
            z[ig, 2 * o : 2 * o + 1, :] = jnp.sum(real, axis=0, keepdims=True)
            z[ig, 2 * o + 1 : 2 * o + 2, :] = jnp.sum(imag, axis=0, keepdims=True)
        return carry

    lax.fori_loop(0, lat_dev * groups, other_rows, 0)

    @pl.when(has_high)
    def _():
        up.wait_send()

    @pl.when(has_low)
    def _():
        down.wait_send()

    by_order = z[...].reshape(128, deg).T.astype(bf16)
    send_a[...] = by_order.reshape(y_count, zc_count * 2, 128)

    @pl.when(is_high)
    def _():
        pl.semaphore_wait(barrier, y_count - 1 + Z - 1)
        tell(far, lat - 1, lon)

    @pl.when(is_low)
    def _():
        pl.semaphore_wait(far, 1)

    a_copies = [
        pltpu.make_async_remote_copy(
            src_ref=send_a.at[t],
            dst_ref=recv_a.at[y],
            send_sem=sem_a_s.at[t],
            recv_sem=sem_a_r.at[y],
            device_id=(t * zc_count + zc, lon),
            device_id_type=MESH,
        )
        for t in range(y_count)
    ]
    for t in corner_first(y_count):
        pl.when(t != y)(a_copies[t].start)
    recv_a[y] = send_a[y]

    fetches[8].wait()
    fetches[9].wait()
    half = lax.broadcasted_iota(jnp.int32, (8, lat_parts), 0) // lat_dev
    orders = (2 * lat + half).astype(f32)
    order_square = orders * orders
    cosine, log_sine, weight = per_lat[0], per_lat[1], per_lat[2]
    norm = jnp.where(half == 0, scalars[2 * deg + 2 * lat], scalars[2 * deg + 2 * lat + 1])
    start = jnp.exp(norm + orders * log_sine)

    def advance(l, state):
        previous, before, inverse, degree = state
        denominator = degree * degree - order_square
        root = lax.rsqrt(jnp.maximum(denominator, 1.0))
        first = jnp.where(denominator > 0.0, scalars[l] * root, 0.0)
        second = first * inverse
        fresh = first * cosine * previous - second * before
        fresh += jnp.where(denominator == 0.0, start, 0.0)
        table[pl.ds(pl.multiple_of(l * 8, 8), 8), :] = fresh * weight
        inverse = jnp.maximum(denominator, 0.0) * root * scalars[deg + l]
        return fresh, previous, inverse, degree + 1.0

    zeros = cosine * 0.0
    lax.fori_loop(0, deg, advance, (zeros, zeros, zeros, zeros), unroll=8)

    for s in range(8):
        exact = table[pl.ds(s, deg, stride=8), :]
        high = exact.astype(bf16)
        tcat[s, :, :lat_parts] = high
        tcat[s, :, lat_parts:] = (exact - high.astype(f32)).astype(bf16)

    for t in range(y_count):
        pl.when(t != y)(a_copies[t].wait_send)
    for t in range(y_count):
        arrival = pltpu.make_async_copy(recv_a.at[t], recv_a.at[t], sem_a_r.at[t])
        pl.when(t != y)(arrival.wait)

    wide_a[...] = recv_a[...].astype(f32).reshape(deg, 128)
    b_copies = [
        pltpu.make_async_remote_copy(
            src_ref=send_b.at[t],
            dst_ref=recv_b.at[zc],
            send_sem=sem_b_s.at[t],
            recv_sem=sem_b_r.at[zc],
            device_id=(y * zc_count + t, lon),
            device_id_type=MESH,
        )
        for t in range(zc_count)
    ]
    for t in [2 * p + e for p in corner_first(Z) for e in (1, 0)]:
        low = wide_a[pl.ds(2 * t, y_count, stride=2 * zc_count), :]
        high = wide_a[pl.ds(2 * t + 1, y_count, stride=2 * zc_count), :]
        send_b[t] = jnp.concatenate([low, high], axis=0).astype(bf16)
        pl.when(t != zc)(b_copies[t].start)
    recv_b[zc] = send_b[zc]

    for _, copy in lon_copies:
        copy.wait_send()
    for t in range(zc_count):
        arrival = pltpu.make_async_copy(recv_b.at[t], recv_b.at[t], sem_b_r.at[t])
        pl.when(t != zc)(arrival.wait)

    arrived = recv_b[...].astype(f32)
    for m in range(2):
        of_order = arrived[:, m * y_count : (m + 1) * y_count, :].reshape(lat_parts, 128)
        by_lat = of_order.T.astype(bf16)
        total = None
        for i in range(lat_dev):
            part = by_lat[i * 32 : (i + 1) * 32, :]
            part = jnp.concatenate([part, part], axis=1)
            term = lax.dot_general(part, tcat[m * lat_dev + i], NT, preferred_element_type=f32)
            total = term if total is None else total + term
        out[0, :, :, m, :] = total.reshape(chans, 2, deg)

    for t in range(zc_count):
        pl.when(t != zc)(b_copies[t].wait_send)


def body(consts, fields, filter_weights, filter_values, row_offsets, col_offsets, support_sizes):
    _, lat_dev, all_chans, lon_dev = fields.shape
    lat_parts, lon_parts = lax.axis_size("lat"), lax.axis_size("lon")
    chans, deg = all_chans // lon_parts, 2 * lat_parts
    y_count, zc_count = lat_parts // (2 * Z), 2 * Z
    vmem, hbm = pl.BlockSpec(memory_space=pltpu.VMEM), pl.BlockSpec(memory_space=pltpu.HBM)
    f32, bf16, dma = jnp.float32, jnp.bfloat16, pltpu.SemaphoreType.DMA
    return pl.pallas_call(
        kernel,
        out_shape=jax.ShapeDtypeStruct((1, chans, 2, 2, deg), f32),
        in_specs=[hbm] * 10,
        out_specs=vmem,
        scratch_shapes=[
            pltpu.VMEM((SUPPORT, GROUP, all_chans), bf16),
            pltpu.VMEM((lat_dev, SUPPORT), f32),
            pltpu.VMEM((lat_dev, SUPPORT), jnp.int32),
            pltpu.VMEM((lat_dev, SUPPORT), jnp.int32),
            pltpu.SMEM((lat_dev,), jnp.int32),
            pltpu.VMEM((3, 8, lat_parts), f32),
            pltpu.SMEM((3 * deg,), f32),
            pltpu.VMEM((2 * HALF * GROUP, 128), f32),
            pltpu.VMEM((128, 2 * HALF), f32),
            pltpu.VMEM((chans * GROUP, 2 * HALF), f32),
            pltpu.VMEM((chans * GROUP, 2 * HALF), f32),
            pltpu.VMEM((lon_parts, lat_dev, chans, lon_dev), bf16),
            pltpu.VMEM((lon_parts, lon_dev, 2 * deg), bf16),
            pltpu.VMEM((2 * deg, 2 * HALF), bf16),
            pltpu.VMEM((lat_dev, chans, 2 * deg), bf16),
            pltpu.VMEM((2, LAT_REACH, chans, 2 * deg), bf16),
            pltpu.VMEM((lat_dev + 2 * LAT_REACH, chans, 2 * deg), f32),
            pltpu.VMEM((lat_dev, 2 * HALF), f32),
            pltpu.VMEM((lat_dev, 2 * HALF), jnp.int32),
            pltpu.VMEM((lat_dev, 2 * HALF), jnp.int32),
            pltpu.VMEM((ROWS * chans * GROUP, 2 * HALF), bf16),
            pltpu.VMEM((lat_dev, ROWS * chans * GROUP, 2 * deg), f32),
            pltpu.VMEM((lat_dev * chans // GROUP, GROUP * GROUP, 2 * deg), f32),
            pltpu.VMEM((lat_dev * chans // GROUP, 2 * GROUP, deg), f32),
            pltpu.VMEM((y_count, 2 * zc_count, 128), bf16),
            pltpu.VMEM((y_count, 2 * zc_count, 128), bf16),
            pltpu.VMEM((deg, 128), f32),
            pltpu.VMEM((zc_count, 2 * y_count, 128), bf16),
            pltpu.VMEM((zc_count, 2 * y_count, 128), bf16),
            pltpu.VMEM((deg * 8, lat_parts), f32),
            pltpu.VMEM((8, deg, 2 * lat_parts), bf16),
            pltpu.SemaphoreType.REGULAR,
            pltpu.SemaphoreType.REGULAR,
            dma((10,)),
            dma((lon_parts - 1,)),
            dma((lon_parts - 1,)),
            dma((2,)),
            dma((2,)),
            dma((y_count,)),
            dma((y_count,)),
            dma((zc_count,)),
            dma((zc_count,)),
        ],
        compiler_params=pltpu.CompilerParams(
            collective_id=0, has_side_effects=True, vmem_limit_bytes=60 * 1024 * 1024
        ),
    )(
        fields[0], filter_weights.transpose(0, 2, 1), filter_values, row_offsets, col_offsets, support_sizes,
        *(jnp.asarray(c) for c in consts),
    )


def solution(mesh):
    placed = (
        P(None, "lat", None, "lon"),
        P(),
        P("lat", None),
        P("lat", None),
        P("lat", None),
        P("lat"),
    )

    def whole(fields, *rest):
        lat_parts, lon_parts = mesh.shape["lat"], mesh.shape["lon"]
        consts = tables(
            lat_parts, lon_parts, fields.shape[3] // lon_parts, fields.shape[1] // lat_parts
        )
        return jax.shard_map(
            functools.partial(body, consts),
            mesh=mesh,
            in_specs=placed,
            out_specs=P(None, "lon", None, "lat", None),
            check_vma=False,
        )(fields, *rest)

    return whole
```

```python
import functools
import math

import jax
import jax.numpy as jnp
import ml_dtypes
import numpy as np
from jax import lax
from jax.experimental import pallas as pl
from jax.experimental.pallas import tpu as pltpu
from jax.sharding import PartitionSpec as P

GROUP = 8
SUPPORT = 49
LON_REACH = 16
HALF = 64
Z = 8
MESH = pl.DeviceIdType.MESH
NT = (((1,), (1,)), ((), ()))
WIDE = 384
PAIRS = {
    0: (0, 1, 2, 3), 1: (0, 1, 2, 3), 2: (0, 1, 2, 3), 3: (0, 1, 2, 3),
    4: (1, 2, 3), 5: (2, 3), 6: (3,), -1: (0, 1, 2), -2: (0, 1), -3: (0,),
}
FIRST = {i: sum(len(PAIRS[q]) for q in list(PAIRS)[:n]) for n, i in enumerate(PAIRS)}


def far_first(count):
    return sorted(range(1, count), key=lambda d: -min(d, count - d))


def corner_first(count):
    return sorted(range(count), key=lambda t: min(t, count - t))


def split(x):
    high = x.astype(ml_dtypes.bfloat16)
    low = (x - high.astype(np.float64)).astype(ml_dtypes.bfloat16)
    return high, low


def tables(lat_parts, lon_parts, lon_dev, lat_dev):
    nlon, nlat, deg = lon_parts * lon_dev, lat_parts * lat_dev, 2 * lat_parts
    orders = np.arange(deg)
    phase = 2.0 * math.pi / nlon * ((np.arange(nlon)[:, None] * orders[None, :]) % nlon)
    fourier = np.concatenate([np.cos(phase), -np.sin(phase)], 1).astype(ml_dtypes.bfloat16)
    fourier = fourier.reshape(lon_parts, lon_dev, 2 * deg)
    shifts = np.arange(-LON_REACH, LON_REACH + 1)
    turn = 2.0 * math.pi / nlon * ((orders[:, None] * shifts[None, :]) % nlon)
    turn = np.concatenate([np.cos(turn), np.sin(turn)], 0)
    shift_table = np.zeros((2 * deg, 2 * HALF), ml_dtypes.bfloat16)
    shift_table[:, : shifts.size], shift_table[:, HALF : HALF + shifts.size] = split(turn)
    band = np.arange(lat_parts)
    lats = lat_dev * band[None, :] + (np.arange(8) % lat_dev)[:, None]
    colat = math.pi * (lats + 0.5) / nlat
    per_lat = np.stack([np.cos(colat), np.log(np.sin(colat)), math.pi / nlat * np.sin(colat)])
    factors = np.arange(1, deg)
    log_product = np.concatenate([[0.0], np.cumsum(np.log((2.0 * factors - 1) / (2.0 * factors)))])
    log_norm = 0.5 * (np.log((2.0 * orders + 1) / (4 * math.pi)) + log_product)
    grow = np.sqrt(np.maximum(4.0 * orders * orders - 1, 1.0))
    scalars = np.concatenate([grow, 1.0 / grow, log_norm])
    return fourier, shift_table, per_lat.astype(np.float32), scalars.astype(np.float32)


def kernel(
    fields, raw_h, values_h, row_off_h, col_off_h, sizes_h, fourier, shift_table, per_lat_h, scalars_h,
    out,
    raw, values, row_off, col_off, sizes, per_lat, scalars, wide_w, turned, own_turned, weights,
    blocks, four, shift, xs, meta, left, w, z, send_a, recv_a, wide_a, send_b, recv_b, wide_b, natural,
    table, tcat,
    near, far, sem_in, sem_lon_s, sem_lon_r, sem_halo_s, sem_halo_r, sem_a_s, sem_a_r, sem_b_s, sem_b_r,
):
    lat, lon = lax.axis_index("lat"), lax.axis_index("lon")
    lat_parts, lon_parts = lax.axis_size("lat"), lax.axis_size("lon")
    y_count, zc_count = lat_parts // (2 * Z), 2 * Z
    chip, core, y, zc = lat // 2, lat % 2, lat // zc_count, lat % zc_count
    lat_dev, chans = blocks.shape[1], blocks.shape[2]
    deg = 2 * lat_parts
    f32, bf16 = jnp.float32, jnp.bfloat16

    barrier = pltpu.get_barrier_semaphore()
    is_low, is_high = core == 0, core == 1
    has_low, has_high = lat > 0, lat < lat_parts - 1

    def tell(sem, to_lat, to_lon):
        pl.semaphore_signal(sem, 1, device_id=(to_lat, to_lon), device_id_type=MESH)

    def ahead(at, step, count):
        return jnp.where(at + step >= count, at + step - count, at + step)

    for d in range(1, lon_parts):
        tell(barrier, lat - core, ahead(lon, d, lon_parts))

    @pl.when(is_high)
    def _():
        tell(barrier, lat - 1, lon)

    @pl.when(is_high & has_high)
    def _():
        tell(barrier, lat + 1, lon)

    @pl.when(is_low & has_low)
    def _():
        tell(barrier, lat - 2, lon)

    @pl.when(is_low)
    def _():
        sides = has_low.astype(jnp.int32) + (lat < lat_parts - 2).astype(jnp.int32)
        pl.semaphore_wait(barrier, 2 * (lon_parts - 1) + 1 + sides)
        tell(near, lat + 1, lon)

    @pl.when(is_high)
    def _():
        pl.semaphore_wait(near, 1)

    lon_copies = []
    for d in (1, lon_parts - 1, 2):
        other = ahead(lon, d, lon_parts)
        copy = pltpu.make_async_remote_copy(
            src_ref=fields.at[:, pl.ds(other * chans, chans), :],
            dst_ref=blocks.at[lon],
            send_sem=sem_lon_s.at[d - 1],
            recv_sem=sem_lon_r.at[d - 1],
            device_id=(lat, other),
            device_id_type=MESH,
        )
        copy.start()
        lon_copies.append((d, copy))

    own_block = fields.at[:, pl.ds(lon * chans, chans), :]
    pairs = (
        (raw_h, raw), (values_h, values), (row_off_h, row_off), (col_off_h, col_off),
        (sizes_h, sizes), (shift_table, shift), (own_block, blocks.at[lon]), (fourier, four),
        (per_lat_h, per_lat), (scalars_h, scalars),
    )
    fetches = [pltpu.make_async_copy(p, q, sem_in.at[n]) for n, (p, q) in enumerate(pairs)]
    for fetch in fetches:
        fetch.start()

    @pl.when(is_low)
    def _():
        for d in far_first(y_count):
            tell(barrier, ahead(y, d, y_count) * zc_count + zc + 1, lon)

    @pl.when(is_high)
    def _():
        for d in far_first(Z):
            tell(barrier, y * zc_count + ahead(zc, 2 * d, zc_count), lon)

    for fetch in fetches[:6]:
        fetch.wait()
    cells = lax.broadcasted_iota(jnp.int32, (lat_dev, SUPPORT), 1)
    own_row = lax.broadcasted_iota(jnp.int32, (lat_dev, SUPPORT), 0)
    size_of = jnp.zeros((lat_dev, SUPPORT), jnp.int32)
    for i in range(lat_dev):
        size_of = jnp.where(own_row == i, sizes[i], size_of)
    live = (cells < size_of).astype(f32)
    meta[1] = jnp.zeros(meta.shape[1:], f32)

    @pl.when(jnp.logical_not(has_low))
    def _():
        meta[0] = jnp.zeros(meta.shape[1:], f32)

    @pl.when(jnp.logical_not(has_high))
    def _():
        meta[2] = jnp.zeros(meta.shape[1:], f32)

    for at in (0, HALF):
        meta[1, 0:4, at : at + SUPPORT] = values[...] * live
        meta[1, 4:8, at : at + SUPPORT] = row_off[...].astype(f32)
        meta[1, 8:12, at : at + SUPPORT] = col_off[...].astype(f32)
    up = pltpu.make_async_remote_copy(
        src_ref=meta.at[1],
        dst_ref=meta.at[0],
        send_sem=sem_halo_s.at[0],
        recv_sem=sem_halo_r.at[0],
        device_id=(jnp.where(has_high, lat + 1, 0), lon),
        device_id_type=MESH,
    )
    down = pltpu.make_async_remote_copy(
        src_ref=meta.at[1],
        dst_ref=meta.at[2],
        send_sem=sem_halo_s.at[1],
        recv_sem=sem_halo_r.at[1],
        device_id=(jnp.where(has_low, lat - 1, lat_parts - 1), lon),
        device_id_type=MESH,
    )

    @pl.when(has_high)
    def _():
        up.start()

    @pl.when(has_low)
    def _():
        down.start()

    for slot in (2 * lat_dev - 1, 2 * lat_dev):
        z[slot * 2 : slot * 2 + 2] = jnp.zeros((2,) + z.shape[1:], f32)
    natural[...] = jnp.zeros_like(natural)
    wide_w[...] = jnp.zeros_like(wide_w)
    flat = raw[...].astype(f32).reshape(SUPPORT * GROUP, raw.shape[2])
    for at in (0, HALF * GROUP):
        wide_w[at : at + SUPPORT * GROUP, : raw.shape[2]] = flat
    for a in range(GROUP):
        turned[...] = wide_w[pl.ds(a, 2 * HALF, stride=GROUP), :].T
        own_turned[a * chans : (a + 1) * chans, :] = turned[
            pl.ds(pl.multiple_of(lon * chans, chans), chans), :
        ]
    for o in range(chans):
        weights[o * GROUP : (o + 1) * GROUP, :] = own_turned[pl.ds(o, GROUP, stride=chans), :]
    weights_f32 = weights[...]
    shift_row = lax.broadcasted_iota(jnp.int32, (2 * HALF, 2 * HALF), 0)
    shift_lane = lax.broadcasted_iota(jnp.int32, (2 * HALF, 2 * HALF), 1)
    same_half = shift_row // HALF == shift_lane // HALF
    shift_of_row = (shift_row % HALF - LON_REACH).astype(f32)

    def build(i):
        part, row = 1 + (i // lat_dev), i % lat_dev
        effective = (weights_f32 * meta[part, row : row + 1, :]).astype(bf16).astype(f32)
        rows_of = meta[part, 4 + row : 5 + row, :]
        rows = PAIRS[i]
        for n, j in enumerate(rows):
            left[n * 128 : (n + 1) * 128, :] = jnp.where(
                rows_of == float(j - i), effective, 0.0
            ).astype(bf16)
        shift_by = meta[part, 8 + row : 9 + row, :]
        pick = (same_half & (shift_of_row == shift_by)).astype(f32).astype(bf16)
        phases = jnp.dot(shift[...], pick, preferred_element_type=f32).astype(bf16)
        block = FIRST[i]
        w[block : block + len(rows)] = lax.dot_general(
            left[: len(rows) * 128, :], phases, NT, preferred_element_type=f32
        ).reshape(len(rows), 128, 2 * deg)

    def transform(block):
        data = blocks[block].reshape(lat_dev * chans, blocks.shape[3])
        part = jnp.dot(data, four[block], preferred_element_type=f32)
        return part.reshape(lat_dev, chans, 2 * deg)

    for i in range(lat_dev):
        build(i)

    @pl.when(has_low)
    def _():
        up.wait_recv()

    @pl.when(has_high)
    def _():
        down.wait_recv()

    for i in PAIRS:
        if not 0 <= i < lat_dev:
            build(i)
    fetches[6].wait()
    fetches[7].wait()
    xs[...] = transform(lon)
    for d, copy in lon_copies:
        copy.wait_recv()
        xs[...] += transform((lon + lon_parts - d) % lon_parts)

    groups = chans // GROUP

    def combine(block, rows, slot, g):
        part = pl.ds(pl.multiple_of(g * GROUP, GROUP), GROUP)
        x_rows = [(xs[j, part, :deg], xs[j, part, deg:]) for j in rows]
        for o in range(GROUP):
            at = pl.multiple_of(g * (GROUP * GROUP), GROUP * GROUP) + o * GROUP
            real = imag = None
            for n, (xr, xi) in enumerate(x_rows):
                tile = w[block + n, pl.ds(at, GROUP), :]
                wr, wi = tile[:, :deg], tile[:, deg:]
                re, im = wr * xr - wi * xi, wr * xi + wi * xr
                real, imag = (re, im) if real is None else (real + re, imag + im)
            z[slot * groups + g, 2 * o : 2 * o + 1, :] = jnp.sum(real, axis=0, keepdims=True)
            z[slot * groups + g, 2 * o + 1 : 2 * o + 2, :] = jnp.sum(imag, axis=0, keepdims=True)

    def own_lats(ig, carry):
        i, g = ig // groups, ig % groups
        combine(i * lat_dev, list(range(lat_dev)), i, g)
        return carry

    def next_lats(g, carry):
        for i, rows in PAIRS.items():
            if not 0 <= i < lat_dev:
                combine(FIRST[i], rows, i if i > 0 else 3 * lat_dev + i, g)
        return carry

    lax.fori_loop(0, lat_dev * groups, own_lats, 0)
    lax.fori_loop(0, groups, next_lats, 0)

    @pl.when(has_high)
    def _():
        up.wait_send()

    @pl.when(has_low)
    def _():
        down.wait_send()

    by_order = z[...].reshape(WIDE, deg).T.astype(bf16)
    send_a[...] = by_order.reshape(y_count, zc_count * 2, WIDE)

    @pl.when(is_high)
    def _():
        pl.semaphore_wait(barrier, y_count - 1 + Z - 1)
        tell(far, lat - 1, lon)

    @pl.when(is_low)
    def _():
        pl.semaphore_wait(far, 1)

    a_copies = [
        pltpu.make_async_remote_copy(
            src_ref=send_a.at[t],
            dst_ref=recv_a.at[y],
            send_sem=sem_a_s.at[t],
            recv_sem=sem_a_r.at[y],
            device_id=(t * zc_count + zc, lon),
            device_id_type=MESH,
        )
        for t in range(y_count)
    ]
    for t in corner_first(y_count):
        pl.when(t != y)(a_copies[t].start)
    recv_a[y] = send_a[y]

    fetches[8].wait()
    fetches[9].wait()
    half = lax.broadcasted_iota(jnp.int32, (8, lat_parts), 0) // lat_dev
    orders = (2 * lat + half).astype(f32)
    order_square = orders * orders
    cosine, log_sine, weight = per_lat[0], per_lat[1], per_lat[2]
    norm = jnp.where(half == 0, scalars[2 * deg + 2 * lat], scalars[2 * deg + 2 * lat + 1])
    start = jnp.exp(norm + orders * log_sine)

    def advance(l, state):
        previous, before, inverse, degree = state
        denominator = degree * degree - order_square
        root = lax.rsqrt(jnp.maximum(denominator, 1.0))
        first = jnp.where(denominator > 0.0, scalars[l] * root, 0.0)
        second = first * inverse
        fresh = first * cosine * previous - second * before
        fresh += jnp.where(denominator == 0.0, start, 0.0)
        table[pl.ds(pl.multiple_of(l * 8, 8), 8), :] = fresh * weight
        inverse = jnp.maximum(denominator, 0.0) * root * scalars[deg + l]
        return fresh, previous, inverse, degree + 1.0

    zeros = cosine * 0.0
    lax.fori_loop(0, deg, advance, (zeros, zeros, zeros, zeros), unroll=8)

    for s in range(8):
        exact = table[pl.ds(s, deg, stride=8), :]
        high = exact.astype(bf16)
        tcat[s, :, :lat_parts] = high
        tcat[s, :, lat_parts:] = (exact - high.astype(f32)).astype(bf16)

    for t in range(y_count):
        pl.when(t != y)(a_copies[t].wait_send)
    for t in range(y_count):
        arrival = pltpu.make_async_copy(recv_a.at[t], recv_a.at[t], sem_a_r.at[t])
        pl.when(t != y)(arrival.wait)

    came_a = recv_a[...].astype(f32).reshape(deg, WIDE)
    for part in range(3):
        wide_a[part] = came_a[:, part * 128 : (part + 1) * 128]
    b_copies = [
        pltpu.make_async_remote_copy(
            src_ref=send_b.at[t],
            dst_ref=recv_b.at[zc],
            send_sem=sem_b_s.at[t],
            recv_sem=sem_b_r.at[zc],
            device_id=(y * zc_count + t, lon),
            device_id_type=MESH,
        )
        for t in range(zc_count)
    ]
    for t in [2 * p + e for p in corner_first(Z) for e in (1, 0)]:
        for part in range(3):
            low = wide_a[part, pl.ds(2 * t, y_count, stride=2 * zc_count), :]
            high = wide_a[part, pl.ds(2 * t + 1, y_count, stride=2 * zc_count), :]
            send_b[t, :, part * 128 : (part + 1) * 128] = jnp.concatenate(
                [low, high], axis=0
            ).astype(bf16)
        pl.when(t != zc)(b_copies[t].start)
    recv_b[zc] = send_b[zc]

    for _, copy in lon_copies:
        copy.wait_send()
    for t in range(zc_count):
        arrival = pltpu.make_async_copy(recv_b.at[t], recv_b.at[t], sem_b_r.at[t])
        pl.when(t != zc)(arrival.wait)

    came_b = recv_b[...].astype(f32).reshape(deg, WIDE)
    for part in range(3):
        wide_b[part] = came_b[:, part * 128 : (part + 1) * 128]
    for m in range(2):
        for t in range(y_count):
            for part in range(3):
                natural[m, part, 8 + t * zc_count : 8 + (t + 1) * zc_count, :] = wide_b[
                    part, pl.ds(m * y_count + t, zc_count, stride=2 * y_count), :
                ]
        of_order = (
            natural[m, 0, 8 : 8 + lat_parts, :]
            + natural[m, 1, 7 : 7 + lat_parts, :]
            + natural[m, 2, 9 : 9 + lat_parts, :]
        )
        by_lat = of_order.T
        total = None
        for i in range(lat_dev):
            exact = by_lat[i * 32 : (i + 1) * 32, :]
            high = exact.astype(bf16)
            low = (exact - high.astype(f32)).astype(bf16)
            both, factor = jnp.concatenate([high, high], axis=1), m * lat_dev + i
            term = lax.dot_general(both, tcat[factor], NT, preferred_element_type=f32)
            term += lax.dot_general(
                low, tcat[factor, :, :lat_parts], NT, preferred_element_type=f32
            )
            total = term if total is None else total + term
        out[0, :, :, m, :] = total.reshape(chans, 2, deg)

    for t in range(zc_count):
        pl.when(t != zc)(b_copies[t].wait_send)


def body(consts, fields, filter_weights, filter_values, row_offsets, col_offsets, support_sizes):
    _, lat_dev, all_chans, lon_dev = fields.shape
    lat_parts, lon_parts = lax.axis_size("lat"), lax.axis_size("lon")
    chans, deg = all_chans // lon_parts, 2 * lat_parts
    y_count, zc_count = lat_parts // (2 * Z), 2 * Z
    vmem, hbm = pl.BlockSpec(memory_space=pltpu.VMEM), pl.BlockSpec(memory_space=pltpu.HBM)
    f32, bf16, dma = jnp.float32, jnp.bfloat16, pltpu.SemaphoreType.DMA
    return pl.pallas_call(
        kernel,
        out_shape=jax.ShapeDtypeStruct((1, chans, 2, 2, deg), f32),
        in_specs=[hbm] * 10,
        out_specs=vmem,
        scratch_shapes=[
            pltpu.VMEM((SUPPORT, GROUP, all_chans), bf16),
            pltpu.VMEM((lat_dev, SUPPORT), f32),
            pltpu.VMEM((lat_dev, SUPPORT), jnp.int32),
            pltpu.VMEM((lat_dev, SUPPORT), jnp.int32),
            pltpu.SMEM((lat_dev,), jnp.int32),
            pltpu.VMEM((3, 8, lat_parts), f32),
            pltpu.SMEM((3 * deg,), f32),
            pltpu.VMEM((2 * HALF * GROUP, 128), f32),
            pltpu.VMEM((128, 2 * HALF), f32),
            pltpu.VMEM((chans * GROUP, 2 * HALF), f32),
            pltpu.VMEM((chans * GROUP, 2 * HALF), f32),
            pltpu.VMEM((lon_parts, lat_dev, chans, lon_dev), bf16),
            pltpu.VMEM((lon_parts, lon_dev, 2 * deg), bf16),
            pltpu.VMEM((2 * deg, 2 * HALF), bf16),
            pltpu.VMEM((lat_dev, chans, 2 * deg), f32),
            pltpu.VMEM((3, 16, 2 * HALF), f32),
            pltpu.VMEM((lat_dev * 128, 2 * HALF), bf16),
            pltpu.VMEM((28, 128, 2 * deg), f32),
            pltpu.VMEM((3 * lat_dev * chans // GROUP, 2 * GROUP, deg), f32),
            pltpu.VMEM((y_count, 2 * zc_count, WIDE), bf16),
            pltpu.VMEM((y_count, 2 * zc_count, WIDE), bf16),
            pltpu.VMEM((3, deg, 128), f32),
            pltpu.VMEM((zc_count, 2 * y_count, WIDE), bf16),
            pltpu.VMEM((zc_count, 2 * y_count, WIDE), bf16),
            pltpu.VMEM((3, deg, 128), f32),
            pltpu.VMEM((2, 3, lat_parts + 16, 128), f32),
            pltpu.VMEM((deg * 8, lat_parts), f32),
            pltpu.VMEM((8, deg, 2 * lat_parts), bf16),
            pltpu.SemaphoreType.REGULAR,
            pltpu.SemaphoreType.REGULAR,
            dma((10,)),
            dma((lon_parts - 1,)),
            dma((lon_parts - 1,)),
            dma((2,)),
            dma((2,)),
            dma((y_count,)),
            dma((y_count,)),
            dma((zc_count,)),
            dma((zc_count,)),
        ],
        compiler_params=pltpu.CompilerParams(
            collective_id=0, has_side_effects=True, vmem_limit_bytes=60 * 1024 * 1024
        ),
    )(
        fields[0], filter_weights.transpose(0, 2, 1), filter_values, row_offsets, col_offsets, support_sizes,
        *(jnp.asarray(c) for c in consts),
    )


def solution(mesh):
    placed = (
        P(None, "lat", None, "lon"),
        P(),
        P("lat", None),
        P("lat", None),
        P("lat", None),
        P("lat"),
    )

    def whole(fields, *rest):
        lat_parts, lon_parts = mesh.shape["lat"], mesh.shape["lon"]
        consts = tables(
            lat_parts, lon_parts, fields.shape[3] // lon_parts, fields.shape[1] // lat_parts
        )
        return jax.shard_map(
            functools.partial(body, consts),
            mesh=mesh,
            in_specs=placed,
            out_specs=P(None, "lon", None, "lat", None),
            check_vma=False,
        )(fields, *rest)

    return whole
```

```python
import functools
import math

import jax
import jax.numpy as jnp
import ml_dtypes
import numpy as np
from jax import lax
from jax.experimental import pallas as pl
from jax.experimental.pallas import tpu as pltpu
from jax.sharding import PartitionSpec as P

GROUP = 8
SUPPORT = 49
LON_REACH = 16
HALF = 64
Z = 8
MESH = pl.DeviceIdType.MESH
NT = (((1,), (1,)), ((), ()))
WIDE = 384
PAIRS = {
    0: (0, 1, 2, 3), 1: (0, 1, 2, 3), 2: (0, 1, 2, 3), 3: (0, 1, 2, 3),
    4: (1, 2, 3), 5: (2, 3), 6: (3,), -1: (0, 1, 2), -2: (0, 1), -3: (0,),
}
FIRST = {i: sum(len(PAIRS[q]) for q in list(PAIRS)[:n]) for n, i in enumerate(PAIRS)}


def far_first(count):
    return sorted(range(1, count), key=lambda d: -min(d, count - d))


def corner_first(count):
    return sorted(range(count), key=lambda t: min(t, count - t))


def split(x):
    high = x.astype(ml_dtypes.bfloat16)
    low = (x - high.astype(np.float64)).astype(ml_dtypes.bfloat16)
    return high, low


def tables(lat_parts, lon_parts, lon_dev, lat_dev):
    nlon, nlat, deg = lon_parts * lon_dev, lat_parts * lat_dev, 2 * lat_parts
    orders = np.arange(deg)
    phase = 2.0 * math.pi / nlon * ((np.arange(nlon)[:, None] * orders[None, :]) % nlon)
    fourier = np.concatenate([np.cos(phase), -np.sin(phase)], 1).astype(ml_dtypes.bfloat16)
    fourier = fourier.reshape(lon_parts, lon_dev, 2 * deg)
    shifts = np.arange(-LON_REACH, LON_REACH + 1)
    turn = 2.0 * math.pi / nlon * ((orders[:, None] * shifts[None, :]) % nlon)
    turn = np.concatenate([np.cos(turn), np.sin(turn)], 0)
    shift_table = np.zeros((2 * deg, 2 * HALF), ml_dtypes.bfloat16)
    shift_table[:, : shifts.size], shift_table[:, HALF : HALF + shifts.size] = split(turn)
    band = np.arange(lat_parts)
    lats = lat_dev * band[None, :] + (np.arange(8) % lat_dev)[:, None]
    colat = math.pi * (lats + 0.5) / nlat
    per_lat = np.stack([np.cos(colat), np.log(np.sin(colat)), math.pi / nlat * np.sin(colat)])
    factors = np.arange(1, deg)
    log_product = np.concatenate([[0.0], np.cumsum(np.log((2.0 * factors - 1) / (2.0 * factors)))])
    log_norm = 0.5 * (np.log((2.0 * orders + 1) / (4 * math.pi)) + log_product)
    grow = np.sqrt(np.maximum(4.0 * orders * orders - 1, 1.0))
    scalars = np.concatenate([grow, 1.0 / grow, log_norm])
    return fourier, shift_table, per_lat.astype(np.float32), scalars.astype(np.float32)


def kernel(
    fields, raw_h, values_h, row_off_h, col_off_h, sizes_h, fourier, shift_table, per_lat_h, scalars_h,
    out,
    raw, values, row_off, col_off, sizes, per_lat, scalars, wide_w, turned, own_turned, weights,
    blocks, four, shift, xs, meta, left, w, z, send_a, recv_a, wide_a, send_b, recv_b, wide_b, natural,
    table, tcat,
    near, far, sem_in, sem_lon_s, sem_lon_r, sem_halo_s, sem_halo_r, sem_a_s, sem_a_r, sem_b_s, sem_b_r,
):
    lat, lon = lax.axis_index("lat"), lax.axis_index("lon")
    lat_parts, lon_parts = lax.axis_size("lat"), lax.axis_size("lon")
    y_count, zc_count = lat_parts // (2 * Z), 2 * Z
    chip, core, y, zc = lat // 2, lat % 2, lat // zc_count, lat % zc_count
    lat_dev, chans = blocks.shape[1], blocks.shape[2]
    deg = 2 * lat_parts
    f32, bf16 = jnp.float32, jnp.bfloat16

    barrier = pltpu.get_barrier_semaphore()
    is_low, is_high = core == 0, core == 1
    has_low, has_high = lat > 0, lat < lat_parts - 1

    def tell(sem, to_lat, to_lon):
        pl.semaphore_signal(sem, 1, device_id=(to_lat, to_lon), device_id_type=MESH)

    def ahead(at, step, count):
        return jnp.where(at + step >= count, at + step - count, at + step)

    for d in range(1, lon_parts):
        tell(barrier, lat - core, ahead(lon, d, lon_parts))

    @pl.when(is_high)
    def _():
        tell(barrier, lat - 1, lon)

    @pl.when(is_high & has_high)
    def _():
        tell(barrier, lat + 1, lon)

    @pl.when(is_low & has_low)
    def _():
        tell(barrier, lat - 2, lon)

    @pl.when(is_low)
    def _():
        sides = has_low.astype(jnp.int32) + (lat < lat_parts - 2).astype(jnp.int32)
        pl.semaphore_wait(barrier, 2 * (lon_parts - 1) + 1 + sides)
        tell(near, lat + 1, lon)

    @pl.when(is_high)
    def _():
        pl.semaphore_wait(near, 1)

    lon_copies = []
    for d in (1, lon_parts - 1, 2):
        other = ahead(lon, d, lon_parts)
        copy = pltpu.make_async_remote_copy(
            src_ref=fields.at[:, pl.ds(other * chans, chans), :],
            dst_ref=blocks.at[lon],
            send_sem=sem_lon_s.at[d - 1],
            recv_sem=sem_lon_r.at[d - 1],
            device_id=(lat, other),
            device_id_type=MESH,
        )
        copy.start()
        lon_copies.append((d, copy))

    own_block = fields.at[:, pl.ds(lon * chans, chans), :]
    pairs = (
        (raw_h, raw), (values_h, values), (row_off_h, row_off), (col_off_h, col_off),
        (sizes_h, sizes), (shift_table, shift), (own_block, blocks.at[lon]), (fourier, four),
        (per_lat_h, per_lat), (scalars_h, scalars),
    )
    fetches = [pltpu.make_async_copy(p, q, sem_in.at[n]) for n, (p, q) in enumerate(pairs)]
    for fetch in fetches:
        fetch.start()

    @pl.when(is_low)
    def _():
        for d in far_first(y_count):
            tell(barrier, ahead(y, d, y_count) * zc_count + zc + 1, lon)

    @pl.when(is_high)
    def _():
        for d in far_first(Z):
            tell(barrier, y * zc_count + ahead(zc, 2 * d, zc_count), lon)

    for fetch in fetches[:6]:
        fetch.wait()
    cells = lax.broadcasted_iota(jnp.int32, (lat_dev, SUPPORT), 1)
    own_row = lax.broadcasted_iota(jnp.int32, (lat_dev, SUPPORT), 0)
    size_of = jnp.zeros((lat_dev, SUPPORT), jnp.int32)
    for i in range(lat_dev):
        size_of = jnp.where(own_row == i, sizes[i], size_of)
    live = (cells < size_of).astype(f32)
    meta[1] = jnp.zeros(meta.shape[1:], f32)

    @pl.when(jnp.logical_not(has_low))
    def _():
        meta[0] = jnp.zeros(meta.shape[1:], f32)

    @pl.when(jnp.logical_not(has_high))
    def _():
        meta[2] = jnp.zeros(meta.shape[1:], f32)

    for at in (0, HALF):
        meta[1, 0:4, at : at + SUPPORT] = values[...] * live
        meta[1, 4:8, at : at + SUPPORT] = row_off[...].astype(f32)
        meta[1, 8:12, at : at + SUPPORT] = col_off[...].astype(f32)
    up = pltpu.make_async_remote_copy(
        src_ref=meta.at[1],
        dst_ref=meta.at[0],
        send_sem=sem_halo_s.at[0],
        recv_sem=sem_halo_r.at[0],
        device_id=(jnp.where(has_high, lat + 1, 0), lon),
        device_id_type=MESH,
    )
    down = pltpu.make_async_remote_copy(
        src_ref=meta.at[1],
        dst_ref=meta.at[2],
        send_sem=sem_halo_s.at[1],
        recv_sem=sem_halo_r.at[1],
        device_id=(jnp.where(has_low, lat - 1, lat_parts - 1), lon),
        device_id_type=MESH,
    )

    @pl.when(has_high)
    def _():
        up.start()

    @pl.when(has_low)
    def _():
        down.start()

    for slot in (2 * lat_dev - 1, 2 * lat_dev):
        z[:, slot * 2 : slot * 2 + 2] = jnp.zeros((2, 2) + z.shape[2:], f32)
    natural[...] = jnp.zeros_like(natural)
    wide_w[...] = jnp.zeros_like(wide_w)
    flat = raw[...].astype(f32).reshape(SUPPORT * GROUP, raw.shape[2])
    for at in (0, HALF * GROUP):
        wide_w[at : at + SUPPORT * GROUP, : raw.shape[2]] = flat
    for a in range(GROUP):
        turned[...] = wide_w[pl.ds(a, 2 * HALF, stride=GROUP), :].T
        own_turned[a * chans : (a + 1) * chans, :] = turned[
            pl.ds(pl.multiple_of(lon * chans, chans), chans), :
        ]
    for o in range(chans):
        weights[o * GROUP : (o + 1) * GROUP, :] = own_turned[pl.ds(o, GROUP, stride=chans), :]
    weights_f32 = weights[...]
    shift_row = lax.broadcasted_iota(jnp.int32, (2 * HALF, 2 * HALF), 0)
    shift_lane = lax.broadcasted_iota(jnp.int32, (2 * HALF, 2 * HALF), 1)
    same_half = shift_row // HALF == shift_lane // HALF
    shift_of_row = (shift_row % HALF - LON_REACH).astype(f32)

    def build(i):
        part, row = 1 + (i // lat_dev), i % lat_dev
        effective = (weights_f32 * meta[part, row : row + 1, :]).astype(bf16).astype(f32)
        rows_of = meta[part, 4 + row : 5 + row, :]
        rows = PAIRS[i]
        for n, j in enumerate(rows):
            left[n * 128 : (n + 1) * 128, :] = jnp.where(
                rows_of == float(j - i), effective, 0.0
            ).astype(bf16)
        shift_by = meta[part, 8 + row : 9 + row, :]
        pick = (same_half & (shift_of_row == shift_by)).astype(f32).astype(bf16)
        phases = jnp.dot(shift[...], pick, preferred_element_type=f32).astype(bf16)
        block = FIRST[i]
        w[block : block + len(rows)] = lax.dot_general(
            left[: len(rows) * 128, :], phases, NT, preferred_element_type=f32
        ).reshape(len(rows), 128, 2 * deg)

    def transform(block):
        data = blocks[block].reshape(lat_dev * chans, blocks.shape[3])
        part = jnp.dot(data, four[block], preferred_element_type=f32)
        return part.reshape(lat_dev, chans, 2 * deg)

    for i in range(lat_dev):
        build(i)

    @pl.when(has_low)
    def _():
        up.wait_recv()

    @pl.when(has_high)
    def _():
        down.wait_recv()

    for i in PAIRS:
        if not 0 <= i < lat_dev:
            build(i)
    fetches[6].wait()
    fetches[7].wait()
    xs[...] = transform(lon)
    for d, copy in lon_copies:
        copy.wait_recv()
        xs[...] += transform((lon + lon_parts - d) % lon_parts)

    groups = chans // GROUP

    width = deg // 2

    def gather_sums(tiles):
        place = lax.broadcasted_iota(jnp.int32, tiles[0].shape, 0)
        for bit in (4, 2, 1):
            clear = (place // bit) % 2 == 0
            merged = []
            for p, q in zip(tiles[:bit], tiles[bit:]):
                back, forth = pltpu.roll(p, 8 - bit, 0), pltpu.roll(q, bit, 0)
                merged.append(jnp.where(clear, p, q) + jnp.where(clear, back, forth))
            tiles = merged
        return tiles[0]

    def combine(block, rows, slot, g, half):
        part = pl.ds(pl.multiple_of(g * GROUP, GROUP), GROUP)
        re_at = slice(half * width, (half + 1) * width)
        im_at = slice(deg + half * width, deg + (half + 1) * width)
        x_rows = [(xs[j, part, re_at], xs[j, part, im_at]) for j in rows]
        reals, imags = [], []
        for o in range(GROUP):
            at = pl.ds(pl.multiple_of(g * (GROUP * GROUP), GROUP * GROUP) + o * GROUP, GROUP)
            real = imag = None
            for n, (xr, xi) in enumerate(x_rows):
                wr, wi = w[block + n, at, re_at], w[block + n, at, im_at]
                re, im = wr * xr - wi * xi, wr * xi + wi * xr
                real, imag = (re, im) if real is None else (real + re, imag + im)
            reals.append(real)
            imags.append(imag)
        z[half, slot * groups + g, :GROUP, :] = gather_sums(reals)
        z[half, slot * groups + g, GROUP:, :] = gather_sums(imags)

    def all_lats(half):
        def own_lats(ig, carry):
            i, g = ig // groups, ig % groups
            combine(i * lat_dev, list(range(lat_dev)), i, g, half)
            return carry

        def next_lats(g, carry):
            for i, rows in PAIRS.items():
                if not 0 <= i < lat_dev:
                    combine(FIRST[i], rows, i if i > 0 else 3 * lat_dev + i, g, half)
            return carry

        lax.fori_loop(0, lat_dev * groups, own_lats, 0)
        lax.fori_loop(0, groups, next_lats, 0)
        by_order = z[half].reshape(WIDE, width).T.astype(bf16)
        half_y = y_count // 2
        send_a[half * half_y : (half + 1) * half_y] = by_order.reshape(half_y, zc_count * 2, WIDE)

    all_lats(0)

    @pl.when(has_high)
    def _():
        up.wait_send()

    @pl.when(has_low)
    def _():
        down.wait_send()

    @pl.when(is_high)
    def _():
        pl.semaphore_wait(barrier, y_count - 1 + Z - 1)
        tell(far, lat - 1, lon)

    @pl.when(is_low)
    def _():
        pl.semaphore_wait(far, 1)

    a_copies = [
        pltpu.make_async_remote_copy(
            src_ref=send_a.at[t],
            dst_ref=recv_a.at[y],
            send_sem=sem_a_s.at[t],
            recv_sem=sem_a_r.at[y],
            device_id=(t * zc_count + zc, lon),
            device_id_type=MESH,
        )
        for t in range(y_count)
    ]
    for t in corner_first(y_count):
        if t < y_count // 2:
            pl.when(t != y)(a_copies[t].start)
    all_lats(1)
    for t in corner_first(y_count):
        if t >= y_count // 2:
            pl.when(t != y)(a_copies[t].start)
    recv_a[y] = send_a[y]

    fetches[8].wait()
    fetches[9].wait()
    half = lax.broadcasted_iota(jnp.int32, (8, lat_parts), 0) // lat_dev
    orders = (2 * lat + half).astype(f32)
    order_square = orders * orders
    cosine, log_sine, weight = per_lat[0], per_lat[1], per_lat[2]
    norm = jnp.where(half == 0, scalars[2 * deg + 2 * lat], scalars[2 * deg + 2 * lat + 1])
    start = jnp.exp(norm + orders * log_sine)

    def advance(l, state):
        previous, before, inverse, degree = state
        denominator = degree * degree - order_square
        root = lax.rsqrt(jnp.maximum(denominator, 1.0))
        first = jnp.where(denominator > 0.0, scalars[l] * root, 0.0)
        second = first * inverse
        fresh = first * cosine * previous - second * before
        fresh += jnp.where(denominator == 0.0, start, 0.0)
        table[pl.ds(pl.multiple_of(l * 8, 8), 8), :] = fresh * weight
        inverse = jnp.maximum(denominator, 0.0) * root * scalars[deg + l]
        return fresh, previous, inverse, degree + 1.0

    zeros = cosine * 0.0
    lax.fori_loop(0, deg, advance, (zeros, zeros, zeros, zeros), unroll=8)

    for s in range(8):
        exact = table[pl.ds(s, deg, stride=8), :]
        high = exact.astype(bf16)
        tcat[s, :, :lat_parts] = high
        tcat[s, :, lat_parts:] = (exact - high.astype(f32)).astype(bf16)

    for t in range(y_count):
        pl.when(t != y)(a_copies[t].wait_send)
    for t in range(y_count):
        arrival = pltpu.make_async_copy(recv_a.at[t], recv_a.at[t], sem_a_r.at[t])
        pl.when(t != y)(arrival.wait)

    came_a = recv_a[...].astype(f32).reshape(deg, WIDE)
    for part in range(3):
        wide_a[part] = came_a[:, part * 128 : (part + 1) * 128]
    b_copies = [
        pltpu.make_async_remote_copy(
            src_ref=send_b.at[t],
            dst_ref=recv_b.at[zc],
            send_sem=sem_b_s.at[t],
            recv_sem=sem_b_r.at[zc],
            device_id=(y * zc_count + t, lon),
            device_id_type=MESH,
        )
        for t in range(zc_count)
    ]
    for t in [2 * p + e for p in corner_first(Z) for e in (1, 0)]:
        for part in range(3):
            low = wide_a[part, pl.ds(2 * t, y_count, stride=2 * zc_count), :]
            high = wide_a[part, pl.ds(2 * t + 1, y_count, stride=2 * zc_count), :]
            send_b[t, :, part * 128 : (part + 1) * 128] = jnp.concatenate(
                [low, high], axis=0
            ).astype(bf16)
        pl.when(t != zc)(b_copies[t].start)
    recv_b[zc] = send_b[zc]

    for _, copy in lon_copies:
        copy.wait_send()
    for t in range(zc_count):
        arrival = pltpu.make_async_copy(recv_b.at[t], recv_b.at[t], sem_b_r.at[t])
        pl.when(t != zc)(arrival.wait)

    came_b = recv_b[...].astype(f32).reshape(deg, WIDE)
    for part in range(3):
        wide_b[part] = came_b[:, part * 128 : (part + 1) * 128]
    for m in range(2):
        for t in range(y_count):
            for part in range(3):
                natural[m, part, 8 + t * zc_count : 8 + (t + 1) * zc_count, :] = wide_b[
                    part, pl.ds(m * y_count + t, zc_count, stride=2 * y_count), :
                ]
        of_order = (
            natural[m, 0, 8 : 8 + lat_parts, :]
            + natural[m, 1, 7 : 7 + lat_parts, :]
            + natural[m, 2, 9 : 9 + lat_parts, :]
        )
        by_lat = of_order.T
        total = None
        for i in range(lat_dev):
            exact = by_lat[i * 32 : (i + 1) * 32, :]
            high = exact.astype(bf16)
            low = (exact - high.astype(f32)).astype(bf16)
            both, factor = jnp.concatenate([high, high], axis=1), m * lat_dev + i
            term = lax.dot_general(both, tcat[factor], NT, preferred_element_type=f32)
            term += lax.dot_general(
                low, tcat[factor, :, :lat_parts], NT, preferred_element_type=f32
            )
            total = term if total is None else total + term
        for g in range(groups):
            for p in range(2):
                at = (g * 2 + p) * GROUP
                out[0, g * GROUP : (g + 1) * GROUP, p, m, :] = total[at : at + GROUP, :]

    for t in range(zc_count):
        pl.when(t != zc)(b_copies[t].wait_send)


def body(consts, fields, filter_weights, filter_values, row_offsets, col_offsets, support_sizes):
    _, lat_dev, all_chans, lon_dev = fields.shape
    lat_parts, lon_parts = lax.axis_size("lat"), lax.axis_size("lon")
    chans, deg = all_chans // lon_parts, 2 * lat_parts
    y_count, zc_count = lat_parts // (2 * Z), 2 * Z
    vmem, hbm = pl.BlockSpec(memory_space=pltpu.VMEM), pl.BlockSpec(memory_space=pltpu.HBM)
    f32, bf16, dma = jnp.float32, jnp.bfloat16, pltpu.SemaphoreType.DMA
    return pl.pallas_call(
        kernel,
        out_shape=jax.ShapeDtypeStruct((1, chans, 2, 2, deg), f32),
        in_specs=[hbm] * 10,
        out_specs=vmem,
        scratch_shapes=[
            pltpu.VMEM((SUPPORT, GROUP, all_chans), bf16),
            pltpu.VMEM((lat_dev, SUPPORT), f32),
            pltpu.VMEM((lat_dev, SUPPORT), jnp.int32),
            pltpu.VMEM((lat_dev, SUPPORT), jnp.int32),
            pltpu.SMEM((lat_dev,), jnp.int32),
            pltpu.VMEM((3, 8, lat_parts), f32),
            pltpu.SMEM((3 * deg,), f32),
            pltpu.VMEM((2 * HALF * GROUP, 128), f32),
            pltpu.VMEM((128, 2 * HALF), f32),
            pltpu.VMEM((chans * GROUP, 2 * HALF), f32),
            pltpu.VMEM((chans * GROUP, 2 * HALF), f32),
            pltpu.VMEM((lon_parts, lat_dev, chans, lon_dev), bf16),
            pltpu.VMEM((lon_parts, lon_dev, 2 * deg), bf16),
            pltpu.VMEM((2 * deg, 2 * HALF), bf16),
            pltpu.VMEM((lat_dev, chans, 2 * deg), f32),
            pltpu.VMEM((3, 16, 2 * HALF), f32),
            pltpu.VMEM((lat_dev * 128, 2 * HALF), bf16),
            pltpu.VMEM((28, 128, 2 * deg), f32),
            pltpu.VMEM((2, 3 * lat_dev * chans // GROUP, 2 * GROUP, deg // 2), f32),
            pltpu.VMEM((y_count, 2 * zc_count, WIDE), bf16),
            pltpu.VMEM((y_count, 2 * zc_count, WIDE), bf16),
            pltpu.VMEM((3, deg, 128), f32),
            pltpu.VMEM((zc_count, 2 * y_count, WIDE), bf16),
            pltpu.VMEM((zc_count, 2 * y_count, WIDE), bf16),
            pltpu.VMEM((3, deg, 128), f32),
            pltpu.VMEM((2, 3, lat_parts + 16, 128), f32),
            pltpu.VMEM((deg * 8, lat_parts), f32),
            pltpu.VMEM((8, deg, 2 * lat_parts), bf16),
            pltpu.SemaphoreType.REGULAR,
            pltpu.SemaphoreType.REGULAR,
            dma((10,)),
            dma((lon_parts - 1,)),
            dma((lon_parts - 1,)),
            dma((2,)),
            dma((2,)),
            dma((y_count,)),
            dma((y_count,)),
            dma((zc_count,)),
            dma((zc_count,)),
        ],
        compiler_params=pltpu.CompilerParams(
            collective_id=0, has_side_effects=True, vmem_limit_bytes=60 * 1024 * 1024
        ),
    )(
        fields[0], filter_weights.transpose(0, 2, 1), filter_values, row_offsets, col_offsets, support_sizes,
        *(jnp.asarray(c) for c in consts),
    )


def solution(mesh):
    placed = (
        P(None, "lat", None, "lon"),
        P(),
        P("lat", None),
        P("lat", None),
        P("lat", None),
        P("lat"),
    )

    def whole(fields, *rest):
        lat_parts, lon_parts = mesh.shape["lat"], mesh.shape["lon"]
        consts = tables(
            lat_parts, lon_parts, fields.shape[3] // lon_parts, fields.shape[1] // lat_parts
        )
        return jax.shard_map(
            functools.partial(body, consts),
            mesh=mesh,
            in_specs=placed,
            out_specs=P(None, "lon", None, "lat", None),
            check_vma=False,
        )(fields, *rest)

    return whole
```
